32 devices in a mesh: parts: 2 (over y), expert: 16 (over z, x, core), replica: 1.
Axes of the slice: x: 2, y: 2, z: 4, core: 2. Of those that a mesh axis runs over, the one named last changes fastest.
Arguments:
- layer_inputs: bfloat16 [4096, 2048], P(('parts', 'expert', 'replica')), parts along dimension 0, may hold values from -12 to 12, as said below
- specialist_picks: int32 [4096, 8], P(('parts', 'expert', 'replica')), parts along dimension 0, may hold values from 0 to 15, all different within a row
- coefficient_lookup_entry: int32 [4096, 8], P(('parts', 'expert', 'replica')), parts along dimension 0, may hold values from 0 to 255
- dispatch_coefficients: bfloat16 [256], replicated, may hold values from 0.019897461 to 0.59765625
- retained_specialist_flags: int32 [16], replicated, may hold values from 0 to 1, as said below
- specialist_quotas: int32 [16], replicated, may hold values from 24 to 48, as said below
- gating_projection: bfloat16 [16, 2048, 768], P('expert', 'replica'), may hold values from -0.125 to 0.125
- raising_projection: bfloat16 [16, 2048, 768], P('expert', 'replica'), may hold values from -0.125 to 0.125
Outputs:
- gram: float32 [32, 768, 768], P(('parts', 'expert'), 'replica'), parts along dimension 0
- self_cross: float32 [32, 768, 768], P(('parts', 'expert'), 'replica'), parts along dimension 0
- merge_cross: float32 [32, 768, 768], P(('parts', 'expert'), 'replica'), parts along dimension 0
The draws below stay inside these ranges and needn't reach their ends.
There are 2 independent parts, one for each index of `parts`. The reference program is written for one: setup_inputs(seed, part) draws one part's arguments, and reference() takes and returns one part's arrays. A program takes and returns all parts, laid end to end along the dimension named above; an argument that names none is the same for every part. Nothing has to cross between parts.
Inputs may be any that keep to these rules, and one draw needn't show every extreme that they name: `layer_inputs`: tokens of order one with row scales that differ. `retained_specialist_flags`: in every pair of experts 2 j and 2 j + 1 at least one is kept; expert 0 is kept and expert 1 is not. `specialist_quotas`: the largest capacity equals 48.
All inputs are finite; a program needn't handle non-finite values.
Results may differ from the reference program's by a relative error of at most 0.012.
Values may be sent and summed in bfloat16 or wider, within the bound.
No kernel may reach another device: no remote copies, remote signals or barrier semaphores. Data moves between devices by JAX's collectives and lax.ppermute only.
A program may use at most 128 MiB of HBM per device.

```python
import math
import jax
import jax.numpy as jnp
from jax import lax

D = 2048
HID = 768
PICKS_EACH_ITEM = 8
LEVELS = 256
ITEMS_IN_SEGMENT = 128
EXPERTS = 16
SLOT = 48
TOKENS = 2048
SLOTS_EXP = 768


def draw_layer_inputs(key, part):
    key = jax.random.fold_in(key, 37)
    key_scale, key_noise = jax.random.split(key, 2)
    row_scale = jnp.exp(jax.random.uniform(key_scale, (TOKENS, 1), jnp.float32, math.log(0.6), math.log(1.0)))
    values = jax.random.normal(key_noise, (TOKENS, D), jnp.float32) * row_scale
    return jnp.clip(values, -12.0, 12.0).astype(jnp.bfloat16)


def draw_retained_specialist_flags(key, part):
    key = jax.random.fold_in(key, 11)
    pair_kind = jax.random.randint(key, (EXPERTS // 2,), 0, 3)
    pair_kind = pair_kind.at[0].set(1)
    first_kept = (pair_kind != 2).astype(jnp.int32)
    second_kept = (pair_kind != 1).astype(jnp.int32)
    return jnp.stack([first_kept, second_kept], axis=1).reshape(EXPERTS).astype(jnp.int32)


def draw_specialist_quotas(key, part):
    key = jax.random.fold_in(key, 23)
    key_base, key_order = jax.random.split(key)
    base_caps = jax.random.randint(key_base, (EXPERTS,), SLOT // 2, SLOT + 1)
    shuffled = jax.random.permutation(key_order, EXPERTS)
    base_caps = base_caps.at[shuffled[0]].set(SLOT).at[shuffled[1]].set(SLOT // 2)
    return base_caps.astype(jnp.int32)


def set_ends(array, rng, smallest, high):
    shape = array.shape
    place = [jax.random.randint(jax.random.fold_in(rng, axis), (), 0, shape[axis]) for axis in range(len(shape))]
    array = array.at[tuple(place)].set(smallest)
    longest = shape.index(max(shape))
    place[longest] = (place[longest] + 1) % shape[longest]
    return array.at[tuple(place)].set(high)


def levels(rng, shape, shards, low, largest):
    def one(position, shards_of):
        heights = jax.random.uniform(jax.random.fold_in(jax.random.fold_in(rng, 6), position), (shards_of,), jnp.float32, low / len(shards), largest / len(shards))
        return jnp.repeat(jnp.exp(heights), shape[position] // shards_of).reshape((-1,) + (1,) * (len(shape) - position - 1))

    gain = one(*shards[0])
    for cut in shards[1:]:
        gain = gain * one(*cut)
    return gain


def distinct(own_key, rows, count, top, lift):
    order = jax.random.permutation(jax.random.fold_in(own_key, 1), count)
    boost = order
    for power in range(3):
        boost = boost * boost // count
    boost = boost * lift // count
    tickets = jax.random.randint(jax.random.fold_in(own_key, 2), (rows, count), 0, 4096) + boost
    sure = jax.random.permutation(jax.random.fold_in(own_key, 3), rows)[jnp.arange(count) % rows]
    tickets = jnp.where(jnp.arange(rows)[:, None] == sure[None, :], 1 << 14, tickets)
    merit = tickets * count + jnp.arange(count)
    return lax.top_k(merit.astype(jnp.int32), top)[1].astype(jnp.int32)


def centred(key, dims, spread, bound, cuts=(), kind=jnp.bfloat16):
    level = levels(key, dims, cuts, -0.22, 0.18) if cuts else 1.0
    result = jax.random.normal(key, dims, jnp.float32) * spread * level
    return jnp.minimum(jnp.maximum(result, -bound), bound).astype(kind)


def setup_inputs(seed: int = 0, part: int = 0) -> dict:
    keys = jax.random.split(jax.random.key(seed), 9)
    part_splits = jax.random.split(jax.random.fold_in(keys[8], part), 9)
    layer_inputs = draw_layer_inputs(jax.random.fold_in(jax.random.fold_in(keys[8], part), 71), part)
    specialist_picks = distinct(part_splits[1], TOKENS, EXPERTS, PICKS_EACH_ITEM, 4096)
    coefficient_lookup_entry = set_ends(jax.random.randint(part_splits[2], (TOKENS, PICKS_EACH_ITEM), 0, LEVELS), jax.random.fold_in(part_splits[2], 1), 0, LEVELS - 1).astype(jnp.int32)
    dispatch_coefficients = jnp.clip(jnp.exp(jax.random.uniform(keys[3], (LEVELS,), jnp.float32, math.log(0.019897461), math.log(0.59765625))), 0.019897461, 0.59765625).astype(jnp.bfloat16)
    retained_specialist_flags = draw_retained_specialist_flags(jax.random.fold_in(keys[8], 71), part)
    specialist_quotas = draw_specialist_quotas(jax.random.fold_in(keys[8], 71), part)
    gating_projection = centred(keys[6], (EXPERTS, D, HID), D ** -0.5, 0.125, ((0, 16),))
    raising_projection = centred(keys[7], (EXPERTS, D, HID), D ** -0.5, 0.125, ((0, 16),))
    return {"layer_inputs": layer_inputs, "specialist_picks": specialist_picks, "coefficient_lookup_entry": coefficient_lookup_entry, "dispatch_coefficients": dispatch_coefficients, "retained_specialist_flags": retained_specialist_flags, "specialist_quotas": specialist_quotas, "gating_projection": gating_projection, "raising_projection": raising_projection}


def hidden_rows(slot_rows, w_gate, w_up):
    gate_out = jnp.dot(slot_rows, w_gate, preferred_element_type=jnp.float32)
    upward = jnp.dot(slot_rows, w_up, preferred_element_type=jnp.float32)
    return (jax.nn.silu(gate_out) * upward).astype(jnp.bfloat16)


def dispatches_at_position(segment_ordinals, specialist_quotas):
    flat_ids = segment_ordinals.reshape(-1)
    route_total = flat_ids.shape[0]
    indicator_vectors = (flat_ids[:, None] == jnp.arange(EXPERTS, dtype=jnp.int32)[None, :]).astype(jnp.int32)
    before = jnp.cumsum(indicator_vectors, axis=0) - indicator_vectors
    route_rank = jnp.sum(before * indicator_vectors, axis=1)
    dispatch_bound = jnp.sum(indicator_vectors * specialist_quotas[None, :], axis=1)
    target = jnp.where(route_rank < dispatch_bound, flat_ids * SLOT + route_rank, EXPERTS * SLOT)
    empty_table = jnp.full((EXPERTS * SLOT,), route_total, jnp.int32)
    return empty_table.at[target].set(jnp.arange(route_total, dtype=jnp.int32), mode="drop")


def weigh_rows(slot_weights, hidden):
    return (slot_weights[:, None].astype(jnp.float32) * hidden.astype(jnp.float32)).astype(jnp.bfloat16)


def expert_stats(own_hidden, own_weighted, crossed, incoming, keep_flag, merge_flag):
    gram_part = keep_flag * jnp.dot(own_hidden.T, own_hidden, preferred_element_type=jnp.float32)
    gram_part = gram_part + merge_flag * jnp.dot(crossed.T, crossed, preferred_element_type=jnp.float32)
    self_part = keep_flag * jnp.dot(own_hidden.T, own_weighted, preferred_element_type=jnp.float32)
    merge_part = merge_flag * jnp.dot(crossed.T, incoming, preferred_element_type=jnp.float32)
    return gram_part, self_part, merge_part


def reference(layer_inputs, specialist_picks, coefficient_lookup_entry, dispatch_coefficients, retained_specialist_flags, specialist_quotas, gating_projection, raising_projection):
    segment_sequence = TOKENS // ITEMS_IN_SEGMENT
    per_block = ITEMS_IN_SEGMENT * PICKS_EACH_ITEM
    dispatch_sequence = jax.vmap(lambda segment_ordinals: dispatches_at_position(segment_ordinals, specialist_quotas))(specialist_picks.reshape(segment_sequence, ITEMS_IN_SEGMENT, PICKS_EACH_ITEM))
    is_valid = dispatch_sequence < per_block
    block_base = (jnp.arange(segment_sequence, dtype=jnp.int32) * ITEMS_IN_SEGMENT)[:, None]
    token_table = jnp.where(is_valid, block_base + dispatch_sequence // PICKS_EACH_ITEM, TOKENS).astype(jnp.int32).reshape(segment_sequence, EXPERTS, SLOT)
    weights = dispatch_coefficients[coefficient_lookup_entry].reshape(segment_sequence, per_block)
    padded_weights = jnp.concatenate([weights, jnp.zeros((segment_sequence, 1), weights.dtype)], axis=1)
    weight_slots = jnp.take_along_axis(padded_weights, dispatch_sequence, axis=1).reshape(segment_sequence, EXPERTS, SLOT)
    padded_tokens = jnp.concatenate([layer_inputs, jnp.zeros((1, D), layer_inputs.dtype)], axis=0)
    mask_float = retained_specialist_flags.astype(jnp.float32)

    def rows_of(expert):
        slot_index = lax.dynamic_index_in_dim(token_table, expert, axis=1, keepdims=False).reshape(-1)
        slot_weights = lax.dynamic_index_in_dim(weight_slots, expert, axis=1, keepdims=False).reshape(-1)
        return padded_tokens[slot_index], slot_weights

    def pair_stats(pair_index):
        first_expert = 2 * pair_index
        second_expert = first_expert + 1
        first_rows, first_weights = rows_of(first_expert)
        second_rows, second_weights = rows_of(second_expert)
        first_own = hidden_rows(first_rows, gating_projection[first_expert], raising_projection[first_expert])
        second_own = hidden_rows(second_rows, gating_projection[second_expert], raising_projection[second_expert])
        first_cross = hidden_rows(second_rows, gating_projection[first_expert], raising_projection[first_expert])
        second_cross = hidden_rows(first_rows, gating_projection[second_expert], raising_projection[second_expert])
        first_weighted = weigh_rows(first_weights, first_own)
        second_weighted = weigh_rows(second_weights, second_own)
        keep_first = mask_float[first_expert]
        keep_second = mask_float[second_expert]
        first_stats = expert_stats(first_own, first_weighted, first_cross, second_weighted,
                                   keep_first, keep_first * (1.0 - keep_second))
        second_stats = expert_stats(second_own, second_weighted, second_cross, first_weighted,
                                    keep_second, keep_second * (1.0 - keep_first))
        return tuple(jnp.stack([one, two]) for one, two in zip(first_stats, second_stats))

    grams, selfs, merges = lax.map(pair_stats, jnp.arange(EXPERTS // 2, dtype=jnp.int32))
    scale_total = jnp.float32(SLOTS_EXP)
    gram = grams.reshape(EXPERTS, HID, HID) / scale_total
    self_cross = selfs.reshape(EXPERTS, HID, HID) / scale_total
    merge_cross = merges.reshape(EXPERTS, HID, HID) / scale_total
    return gram, self_cross, merge_cross
```

```python
import functools

import jax
import jax.numpy as jnp
from jax import lax
from jax.experimental import pallas as pl
from jax.experimental.pallas import tpu as pltpu
from jax.sharding import PartitionSpec as P


def swapped(x, axis, stride):
    return lax.ppermute(x, axis, [(i, i ^ 1 << stride) for i in range(lax.axis_size(axis))])


def hidden_rows(slot_rows, w_gate, w_up):
    gate_out = jnp.einsum("nsd,dh->nsh", slot_rows, w_gate, preferred_element_type=jnp.float32)
    upward = jnp.einsum("nsd,dh->nsh", slot_rows, w_up, preferred_element_type=jnp.float32)
    return (jax.nn.silu(gate_out) * upward).astype(jnp.bfloat16)


def weigh_rows(slot_weights, hidden):
    return (slot_weights[..., None].astype(jnp.float32) * hidden.astype(jnp.float32)).astype(
        jnp.bfloat16
    )


def dispatches_at_position(segment_ordinals, specialist_quotas, position_ordinal):
    specialist_sequence = specialist_quotas.shape[0]
    flat_ids = segment_ordinals.reshape(-1)
    route_total = flat_ids.shape[0]
    indicator_vectors = (
        flat_ids[:, None] == jnp.arange(specialist_sequence, dtype=jnp.int32)[None, :]
    ).astype(jnp.int32)
    before = jnp.cumsum(indicator_vectors, axis=0) - indicator_vectors
    route_rank = jnp.sum(before * indicator_vectors, axis=1)
    dispatch_bound = jnp.sum(indicator_vectors * specialist_quotas[None, :], axis=1)
    target = jnp.where(
        route_rank < dispatch_bound,
        flat_ids * position_ordinal + route_rank,
        specialist_sequence * position_ordinal,
    )
    empty_table = jnp.full((specialist_sequence * position_ordinal,), route_total, jnp.int32)
    return empty_table.at[target].set(jnp.arange(route_total, dtype=jnp.int32), mode="drop")


def shards(
    layer_inputs,
    specialist_picks,
    coefficient_lookup_entry,
    dispatch_coefficients,
    retained_specialist_flags,
    specialist_quotas,
    gating_projection,
    raising_projection,
):
    specialist_sequence = retained_specialist_flags.shape[0]
    replica_count = lax.axis_size("replica")
    tok_rows, top_count = specialist_picks.shape
    model_width = layer_inputs.shape[1]
    position_ordinal = max(4, 3 * tok_rows * top_count // (4 * specialist_sequence))
    own_index = lax.axis_index("expert")
    partner_index = jnp.bitwise_xor(own_index, 1)
    expert_lane = jnp.arange(specialist_sequence, dtype=jnp.int32)
    keep_own = jnp.sum(jnp.where(expert_lane == own_index, retained_specialist_flags, 0))
    keep_partner = jnp.sum(jnp.where(expert_lane == partner_index, retained_specialist_flags, 0))
    keep_flag = keep_own.astype(jnp.bfloat16)
    merge_flag = (keep_own * (1 - keep_partner)).astype(jnp.bfloat16)
    gathered_gate, gathered_up = (
        lax.all_gather(gating_projection, "replica", axis=1, tiled=True),
        lax.all_gather(raising_projection, "replica", axis=1, tiled=True),
    )
    w_gate = gathered_gate[0]
    w_up = gathered_up[0]
    dispatch_sequence = dispatches_at_position(
        specialist_picks, specialist_quotas, position_ordinal
    )
    route_total = tok_rows * top_count
    token_slot = jnp.where(
        dispatch_sequence < route_total, dispatch_sequence // top_count, tok_rows
    )
    padded_tokens = jnp.concatenate(
        [layer_inputs, jnp.zeros((1, model_width), layer_inputs.dtype)], axis=0
    )
    send_rows = padded_tokens[token_slot].reshape(
        specialist_sequence, position_ordinal, model_width
    )
    levels = dispatch_coefficients.shape[0]
    onehot_levels = (
        coefficient_lookup_entry.reshape(-1)[:, None]
        == jnp.arange(levels, dtype=jnp.int32)[None, :]
    ).astype(jnp.bfloat16)
    route_weights = jnp.dot(
        onehot_levels, dispatch_coefficients, preferred_element_type=jnp.float32
    )
    padded_weights = jnp.concatenate([route_weights, jnp.zeros((1,), jnp.float32)], axis=0)
    send_weights = (
        padded_weights[dispatch_sequence]
        .astype(jnp.bfloat16)
        .reshape(specialist_sequence, position_ordinal)
    )
    slot_rows = lax.all_to_all(send_rows, "expert", split_axis=0, concat_axis=0, tiled=True)
    slot_weights = lax.all_to_all(send_weights, "expert", split_axis=0, concat_axis=0, tiled=True)
    own_hidden = hidden_rows(slot_rows, w_gate, w_up)
    arrived, own_hidden, own_weighted = (
        slot_rows,
        own_hidden,
        weigh_rows(slot_weights, own_hidden),
    )
    partner_rows, incoming = swapped((arrived, own_weighted), "expert", 0)
    crossed = hidden_rows(partner_rows, w_gate, w_up)
    hidden_width = own_hidden.shape[-1]
    own_flat = (own_hidden * keep_flag).reshape(-1, hidden_width)
    weighted_flat = own_weighted.reshape(-1, hidden_width)
    crossed_flat = (crossed * merge_flag).reshape(-1, hidden_width)
    incoming_flat = incoming.reshape(-1, hidden_width)
    both_rows = jnp.concatenate([own_flat, crossed_flat], axis=0)
    gram_part = jnp.einsum("mi,mj->ij", both_rows, both_rows, preferred_element_type=jnp.float32)
    self_part = jnp.einsum("mi,mj->ij", own_flat, weighted_flat, preferred_element_type=jnp.float32)
    merge_part = jnp.einsum(
        "mi,mj->ij", crossed_flat, incoming_flat, preferred_element_type=jnp.float32
    )
    shared_rows = lax.psum_scatter(
        jnp.concatenate([gram_part, self_part, merge_part], axis=1),
        "replica",
        scatter_dimension=0,
        tiled=True,
    )
    slot_total = jnp.float32(replica_count * specialist_sequence * position_ordinal)
    shared_rows = shared_rows / slot_total
    gram = shared_rows[:, :hidden_width]
    self_cross = shared_rows[:, hidden_width : 2 * hidden_width]
    merge_cross = shared_rows[:, 2 * hidden_width :]
    return (gram[None], self_cross[None], merge_cross[None])


def route_table_kernel(quota_ref, pick_ref, entry_ref, coef_ref, out_ref):
    tokens, top_count = pick_ref.shape
    experts = out_ref.shape[0]
    levels = coef_ref.shape[1]
    picks = pick_ref[...]
    entries = entry_ref[...]
    coef = coef_ref[...].astype(jnp.float32)
    expert_lane = lax.broadcasted_iota(jnp.int32, (tokens, experts), 1)
    level_lane = lax.broadcasted_iota(jnp.int32, (tokens, levels), 1)
    chosen = jnp.zeros((tokens, experts), jnp.float32)
    weight = jnp.zeros((tokens, experts), jnp.float32)
    for choice in range(top_count):
        level = entries[:, choice : choice + 1] == level_lane
        value = jnp.sum(jnp.where(level, coef, 0.0), axis=1, keepdims=True)
        hit = picks[:, choice : choice + 1] == expert_lane
        chosen = jnp.where(hit, 1.0, chosen)
        weight = jnp.where(hit, value, weight)
    row = lax.broadcasted_iota(jnp.int32, (tokens, tokens), 0)
    col = lax.broadcasted_iota(jnp.int32, (tokens, tokens), 1)

    def over_tokens(values, token_matrix):
        return lax.dot_general(
            values.astype(jnp.bfloat16),
            token_matrix.astype(jnp.bfloat16),
            (((0,), (0,)), ((), ())),
            preferred_element_type=jnp.float32,
        )

    rank = over_tokens(chosen, jnp.where(row < col, 1.0, 0.0))
    weight_rows = over_tokens(weight, jnp.where(row == col, 1.0, 0.0))
    expert_row = lax.broadcasted_iota(jnp.int32, (experts, tokens), 0)
    bound = jnp.zeros((experts, tokens), jnp.float32)
    for expert in range(experts):
        bound = jnp.where(expert_row == expert, quota_ref[expert].astype(jnp.float32), bound)
    used = jnp.where(rank < bound, weight_rows, 0.0).astype(jnp.bfloat16)
    one = lax.broadcasted_iota(jnp.int32, (experts, experts), 0)
    two = lax.broadcasted_iota(jnp.int32, (experts, experts), 1)
    partner = jnp.where(jnp.bitwise_xor(one, 1) == two, 1.0, 0.0).astype(jnp.bfloat16)
    out_ref[:, :tokens] = used
    out_ref[:, tokens:] = jnp.dot(partner, used, preferred_element_type=jnp.float32).astype(
        jnp.bfloat16
    )


def route_table(picks, entries, coefficients, quotas):
    experts = quotas.shape[0]
    tokens = picks.shape[0]
    vmem = pl.BlockSpec(memory_space=pltpu.VMEM)
    return pl.pallas_call(
        route_table_kernel,
        out_shape=jax.ShapeDtypeStruct((experts, 2 * tokens), jnp.bfloat16),
        in_specs=[pl.BlockSpec(memory_space=pltpu.SMEM), vmem, vmem, vmem],
        out_specs=vmem,
        name="route_table",
    )(quotas, picks, entries, coefficients[None, :])


def hidden_kernel(
    pair_total, place_ref, table_ref, *refs
):
    block_refs = refs[: 2 * pair_total]
    gate_ref, up_ref, lhs_ref, count_ref, weigh_ref, rows_ref, coef_ref = refs[2 * pair_total :]
    tokens = block_refs[0].shape[0]

    @pl.when(pl.program_id(0) == 0)
    def _():
        core = place_ref[0]
        keep = place_ref[1].astype(jnp.float32)
        merge = place_ref[2].astype(jnp.float32)
        row = lax.broadcasted_iota(jnp.int32, (tokens, tokens), 0)
        col = lax.broadcasted_iota(jnp.int32, (tokens, tokens), 1)
        for pair in range(pair_total):
            for side in range(2):
                half = core if side == 0 else 1 - core
                start = pl.multiple_of(2 * pair * tokens + half * tokens, tokens)
                rows_ref[pl.ds(start, tokens), :] = block_refs[2 * pair + side][...]
                table = table_ref[place_ref[3 + pair] + side]
                own = jnp.where(row == col, table[0:1, :], 0.0)
                partner = jnp.where(row == col, table[1:2, :], 0.0)
                own = jnp.sum(own, axis=1, keepdims=True)
                partner = jnp.sum(partner, axis=1, keepdims=True)
                count = jnp.where(own > 0.0, keep, 0.0) + jnp.where(partner > 0.0, merge, 0.0)
                fixed = (2 * pair + side) * tokens
                coef_ref[0, fixed : fixed + tokens, :] = jnp.broadcast_to(count, (tokens, 128))
                coef_ref[1, fixed : fixed + tokens, :] = jnp.broadcast_to(own, (tokens, 128))

    gate = jnp.dot(rows_ref[...], gate_ref[...], preferred_element_type=jnp.float32)
    upward = jnp.dot(rows_ref[...], up_ref[...], preferred_element_type=jnp.float32)
    hidden = (gate / (1.0 + jnp.exp(-gate)) * upward).astype(jnp.bfloat16).astype(jnp.float32)
    lhs_ref[...] = hidden.T.astype(jnp.bfloat16)
    for lane in range(0, hidden.shape[1], 128):
        part = hidden[:, lane : lane + 128]
        count_ref[:, lane : lane + 128] = (part * coef_ref[0]).astype(jnp.bfloat16)
        weigh_ref[:, lane : lane + 128] = (part * coef_ref[1]).astype(jnp.bfloat16)


def hidden_parts(place, table, blocks, w_gate, w_up, name):
    pair_total = len(blocks) // 2
    tokens, width = blocks[0].shape
    rows = len(blocks) * tokens
    hidden_width = w_gate.shape[2]
    tile = 256
    whole = pl.BlockSpec((tokens, width), lambda j, place: (0, 0))
    weights = pl.BlockSpec((None, width, tile), lambda j, place: (0, 0, j))
    out_rows = pl.BlockSpec((rows, tile), lambda j, place: (0, j))
    row_shape = jax.ShapeDtypeStruct((rows, hidden_width), jnp.bfloat16)
    return pl.pallas_call(
        functools.partial(hidden_kernel, pair_total),
        out_shape=(
            jax.ShapeDtypeStruct((hidden_width, rows), jnp.bfloat16),
            row_shape,
            row_shape,
        ),
        grid_spec=pltpu.PrefetchScalarGridSpec(
            num_scalar_prefetch=1,
            grid=(hidden_width // tile,),
            in_specs=[
                pl.BlockSpec(table.shape, lambda j, place: (0, 0, 0)),
                *[whole] * len(blocks),
                weights,
                weights,
            ],
            out_specs=(
                pl.BlockSpec((tile, rows), lambda j, place: (j, 0)),
                out_rows,
                out_rows,
            ),
            scratch_shapes=[
                pltpu.VMEM((rows, width), jnp.bfloat16),
                pltpu.VMEM((2, rows, 128), jnp.float32),
            ],
        ),
        compiler_params=pltpu.CompilerParams(vmem_limit_bytes=40 << 20),
        cost_estimate=pl.CostEstimate(
            flops=4 * rows * width * hidden_width,
            bytes_accessed=4 * width * hidden_width + 2 * rows * width + 6 * rows * hidden_width,
            transcendentals=rows * hidden_width,
        ),
        name=name,
    )(place, table, *blocks, w_gate, w_up)


def sums_kernel(set_total, part_total, has_base, divisor, scaled, scale_ref, *refs):
    lhs = refs[:part_total]
    rest = refs[part_total:]
    rhs = [rest[part_total * index : part_total * (index + 1)] for index in range(set_total)]
    rest = rest[part_total * set_total :]
    bases = rest[:set_total] if has_base else [None] * set_total
    outs = rest[-set_total:]
    for index in range(set_total):
        total = bases[index][...] if has_base else None
        for left, right in zip(lhs, rhs[index]):
            term = jnp.dot(left[...], right[...], preferred_element_type=jnp.float32)
            total = term if total is None else total + term
        if scaled:
            total = total * (scale_ref[index].astype(jnp.float32) / divisor)
        outs[index][...] = total


def sums(lhs, rhs_sets, bases, scales, divisor, name):
    hidden_width = lhs[0].shape[0]
    tile = 256
    rows = sum(part.shape[1] for part in lhs)
    scaled = scales is not None
    if scaled:
        shape, out_spec = (1, hidden_width, hidden_width), pl.BlockSpec(
            (None, hidden_width, tile), lambda j, scale: (0, 0, j)
        )
    else:
        scales = jnp.ones((len(rhs_sets),), jnp.int32)
        shape, out_spec = (hidden_width, hidden_width), pl.BlockSpec(
            (hidden_width, tile), lambda j, scale: (0, j)
        )
    operands = list(lhs)
    in_specs = [pl.BlockSpec(part.shape, lambda j, scale: (0, 0)) for part in lhs]
    for parts in rhs_sets:
        operands += parts
        in_specs += [
            pl.BlockSpec((part.shape[0], tile), lambda j, scale: (0, j)) for part in parts
        ]
    for base in bases or ():
        operands.append(base)
        in_specs.append(pl.BlockSpec((hidden_width, tile), lambda j, scale: (0, j)))
    total = len(rhs_sets)
    return pl.pallas_call(
        functools.partial(
            sums_kernel, total, len(lhs), bool(bases), float(divisor), scaled
        ),
        out_shape=[jax.ShapeDtypeStruct(shape, jnp.float32)] * total,
        grid_spec=pltpu.PrefetchScalarGridSpec(
            num_scalar_prefetch=1,
            grid=(hidden_width // tile,),
            in_specs=in_specs,
            out_specs=[out_spec] * total,
        ),
        compiler_params=pltpu.CompilerParams(vmem_limit_bytes=48 << 20),
        cost_estimate=pl.CostEstimate(
            flops=2 * total * rows * hidden_width * hidden_width,
            bytes_accessed=2 * (1 + total) * rows * hidden_width
            + 4 * total * (2 if bases else 1) * hidden_width * hidden_width,
            transcendentals=0,
        ),
        name=name,
    )(scales, *operands)


def gathered_shards(
    layer_inputs,
    specialist_picks,
    coefficient_lookup_entry,
    dispatch_coefficients,
    retained_specialist_flags,
    specialist_quotas,
    gating_projection,
    raising_projection,
):
    experts = retained_specialist_flags.shape[0]
    tok_rows, top_count = specialist_picks.shape
    position_ordinal = max(4, 3 * tok_rows * top_count // (4 * experts))
    me = lax.axis_index("expert")
    core = jnp.bitwise_and(me, 1)
    expert_lane = jnp.arange(experts, dtype=jnp.int32)
    keep = jnp.sum(jnp.where(expert_lane == me, retained_specialist_flags, 0))
    keep_partner = jnp.sum(
        jnp.where(expert_lane == jnp.bitwise_xor(me, 1), retained_specialist_flags, 0)
    )
    merge = keep * (1 - keep_partner)
    groups = experts // 4

    def along(x):
        return lax.ppermute(x, "expert", [(i, (i + 4) % experts) for i in range(experts)])

    def back(steps):
        return jnp.bitwise_and(jnp.remainder(me + experts - 4 * steps, experts), ~1)

    def place(*firsts):
        return jnp.stack([core, keep, merge, *firsts]).astype(jnp.int32)

    def hidden(firsts, blocks, name):
        return hidden_parts(
            place(*firsts), table, blocks, gating_projection, raising_projection, name
        )

    table = route_table(
        specialist_picks, coefficient_lookup_entry, dispatch_coefficients, specialist_quotas
    )
    line = [layer_inputs, along(layer_inputs)]
    side = [swapped(layer_inputs, "expert", 1)]
    other = swapped(layer_inputs, "expert", 0)
    table = lax.all_to_all(table, "expert", split_axis=0, concat_axis=0, tiled=True)
    table = table.astype(jnp.float32).reshape(experts, 2, tok_rows)
    parts = [hidden([back(0)], [layer_inputs, other], "hidden_0")]
    for step in range(1, groups):
        if step < groups - 1:
            line.append(along(line[step]))
        side.append(swapped(line[step], "expert", 1))
        blocks = [
            side[step - 1],
            swapped(side[step - 1], "expert", 0),
            line[step],
            swapped(line[step], "expert", 0),
        ]
        firsts = [jnp.bitwise_xor(back(step - 1), 2), back(step)]
        parts.append(hidden(firsts, blocks, "hidden_%d" % step))
    blocks = [side[groups - 1], swapped(side[groups - 1], "expert", 0)]
    last = hidden([jnp.bitwise_xor(back(groups - 1), 2)], blocks, "hidden_last")
    incoming = [swapped(part[2], "expert", 0) for part in parts]
    early = sums(
        [part[0] for part in parts],
        [[part[1] for part in parts], [part[2] for part in parts], incoming],
        None,
        None,
        1,
        "early_sums",
    )
    divisor = experts * position_ordinal
    arrived = swapped(last[2], "expert", 0)
    one = jnp.ones((), jnp.int32)
    gram, self_cross = sums(
        [last[0]],
        [[last[1]], [last[2]]],
        early[:2],
        jnp.stack([one, keep]).astype(jnp.int32),
        divisor,
        "own_sums",
    )
    (merge_cross,) = sums(
        [last[0]], [[arrived]], early[2:], merge[None].astype(jnp.int32), divisor, "merge_sums"
    )
    return gram, self_cross, merge_cross


def solution(mesh):
    in_specs = (
        P(("parts", "expert", "replica"), None),
        P(("parts", "expert", "replica"), None),
        P(("parts", "expert", "replica"), None),
        P(),
        P(),
        P(),
        P("expert", "replica", None),
        P("expert", "replica", None),
    )
    out_specs = (
        P(("parts", "expert"), "replica", None),
        P(("parts", "expert"), "replica", None),
        P(("parts", "expert"), "replica", None),
    )
    gather_fits = mesh.shape["replica"] == 1 and mesh.shape["expert"] == 16
    body = gathered_shards if gather_fits else shards
    return jax.shard_map(body, mesh=mesh, in_specs=in_specs, out_specs=out_specs, check_vma=False)
```

```python
import functools

import jax
import jax.numpy as jnp
from jax import lax
from jax.experimental import pallas as pl
from jax.experimental.pallas import tpu as pltpu
from jax.sharding import PartitionSpec as P


def swapped(x, axis, stride):
    return lax.ppermute(x, axis, [(i, i ^ 1 << stride) for i in range(lax.axis_size(axis))])


def hidden_rows(slot_rows, w_gate, w_up):
    gate_out = jnp.einsum("nsd,dh->nsh", slot_rows, w_gate, preferred_element_type=jnp.float32)
    upward = jnp.einsum("nsd,dh->nsh", slot_rows, w_up, preferred_element_type=jnp.float32)
    return (jax.nn.silu(gate_out) * upward).astype(jnp.bfloat16)


def weigh_rows(slot_weights, hidden):
    return (slot_weights[..., None].astype(jnp.float32) * hidden.astype(jnp.float32)).astype(
        jnp.bfloat16
    )


def dispatches_at_position(segment_ordinals, specialist_quotas, position_ordinal):
    specialist_sequence = specialist_quotas.shape[0]
    flat_ids = segment_ordinals.reshape(-1)
    route_total = flat_ids.shape[0]
    indicator_vectors = (
        flat_ids[:, None] == jnp.arange(specialist_sequence, dtype=jnp.int32)[None, :]
    ).astype(jnp.int32)
    before = jnp.cumsum(indicator_vectors, axis=0) - indicator_vectors
    route_rank = jnp.sum(before * indicator_vectors, axis=1)
    dispatch_bound = jnp.sum(indicator_vectors * specialist_quotas[None, :], axis=1)
    target = jnp.where(
        route_rank < dispatch_bound,
        flat_ids * position_ordinal + route_rank,
        specialist_sequence * position_ordinal,
    )
    empty_table = jnp.full((specialist_sequence * position_ordinal,), route_total, jnp.int32)
    return empty_table.at[target].set(jnp.arange(route_total, dtype=jnp.int32), mode="drop")


def shards(
    layer_inputs,
    specialist_picks,
    coefficient_lookup_entry,
    dispatch_coefficients,
    retained_specialist_flags,
    specialist_quotas,
    gating_projection,
    raising_projection,
):
    specialist_sequence = retained_specialist_flags.shape[0]
    replica_count = lax.axis_size("replica")
    tok_rows, top_count = specialist_picks.shape
    model_width = layer_inputs.shape[1]
    position_ordinal = max(4, 3 * tok_rows * top_count // (4 * specialist_sequence))
    own_index = lax.axis_index("expert")
    partner_index = jnp.bitwise_xor(own_index, 1)
    expert_lane = jnp.arange(specialist_sequence, dtype=jnp.int32)
    keep_own = jnp.sum(jnp.where(expert_lane == own_index, retained_specialist_flags, 0))
    keep_partner = jnp.sum(jnp.where(expert_lane == partner_index, retained_specialist_flags, 0))
    keep_flag = keep_own.astype(jnp.bfloat16)
    merge_flag = (keep_own * (1 - keep_partner)).astype(jnp.bfloat16)
    gathered_gate, gathered_up = (
        lax.all_gather(gating_projection, "replica", axis=1, tiled=True),
        lax.all_gather(raising_projection, "replica", axis=1, tiled=True),
    )
    w_gate = gathered_gate[0]
    w_up = gathered_up[0]
    dispatch_sequence = dispatches_at_position(
        specialist_picks, specialist_quotas, position_ordinal
    )
    route_total = tok_rows * top_count
    token_slot = jnp.where(
        dispatch_sequence < route_total, dispatch_sequence // top_count, tok_rows
    )
    padded_tokens = jnp.concatenate(
        [layer_inputs, jnp.zeros((1, model_width), layer_inputs.dtype)], axis=0
    )
    send_rows = padded_tokens[token_slot].reshape(
        specialist_sequence, position_ordinal, model_width
    )
    levels = dispatch_coefficients.shape[0]
    onehot_levels = (
        coefficient_lookup_entry.reshape(-1)[:, None]
        == jnp.arange(levels, dtype=jnp.int32)[None, :]
    ).astype(jnp.bfloat16)
    route_weights = jnp.dot(
        onehot_levels, dispatch_coefficients, preferred_element_type=jnp.float32
    )
    padded_weights = jnp.concatenate([route_weights, jnp.zeros((1,), jnp.float32)], axis=0)
    send_weights = (
        padded_weights[dispatch_sequence]
        .astype(jnp.bfloat16)
        .reshape(specialist_sequence, position_ordinal)
    )
    slot_rows = lax.all_to_all(send_rows, "expert", split_axis=0, concat_axis=0, tiled=True)
    slot_weights = lax.all_to_all(send_weights, "expert", split_axis=0, concat_axis=0, tiled=True)
    own_hidden = hidden_rows(slot_rows, w_gate, w_up)
    arrived, own_hidden, own_weighted = (
        slot_rows,
        own_hidden,
        weigh_rows(slot_weights, own_hidden),
    )
    partner_rows, incoming = swapped((arrived, own_weighted), "expert", 0)
    crossed = hidden_rows(partner_rows, w_gate, w_up)
    hidden_width = own_hidden.shape[-1]
    own_flat = (own_hidden * keep_flag).reshape(-1, hidden_width)
    weighted_flat = own_weighted.reshape(-1, hidden_width)
    crossed_flat = (crossed * merge_flag).reshape(-1, hidden_width)
    incoming_flat = incoming.reshape(-1, hidden_width)
    both_rows = jnp.concatenate([own_flat, crossed_flat], axis=0)
    gram_part = jnp.einsum("mi,mj->ij", both_rows, both_rows, preferred_element_type=jnp.float32)
    self_part = jnp.einsum("mi,mj->ij", own_flat, weighted_flat, preferred_element_type=jnp.float32)
    merge_part = jnp.einsum(
        "mi,mj->ij", crossed_flat, incoming_flat, preferred_element_type=jnp.float32
    )
    shared_rows = lax.psum_scatter(
        jnp.concatenate([gram_part, self_part, merge_part], axis=1),
        "replica",
        scatter_dimension=0,
        tiled=True,
    )
    slot_total = jnp.float32(replica_count * specialist_sequence * position_ordinal)
    shared_rows = shared_rows / slot_total
    gram = shared_rows[:, :hidden_width]
    self_cross = shared_rows[:, hidden_width : 2 * hidden_width]
    merge_cross = shared_rows[:, 2 * hidden_width :]
    return (gram[None], self_cross[None], merge_cross[None])


VMEM_GRANT = 60 << 20


def route_table_kernel(quota_ref, pick_ref, entry_ref, coef_ref, out_ref):
    top_count, tokens = pick_ref.shape
    experts = out_ref.shape[0]
    levels = coef_ref.shape[1]
    picks = pick_ref[...]
    entries = entry_ref[...]
    coef = coef_ref[...]
    expert_row = lax.broadcasted_iota(jnp.int32, (experts, tokens), 0)
    level_row = lax.broadcasted_iota(jnp.int32, (levels, tokens), 0)
    chosen = jnp.zeros((experts, tokens), jnp.float32)
    weight = jnp.zeros((experts, tokens), jnp.float32)
    for choice in range(top_count):
        level = jnp.where(entries[choice : choice + 1, :] == level_row, 1.0, 0.0)
        value = jnp.dot(coef, level.astype(jnp.bfloat16), preferred_element_type=jnp.float32)
        hit = picks[choice : choice + 1, :] == expert_row
        chosen = jnp.where(hit, 1.0, chosen)
        weight = jnp.where(hit, value, weight)
    row = lax.broadcasted_iota(jnp.int32, (tokens, tokens), 0)
    col = lax.broadcasted_iota(jnp.int32, (tokens, tokens), 1)
    earlier = jnp.where(row < col, 1.0, 0.0).astype(jnp.bfloat16)
    rank = jnp.dot(chosen.astype(jnp.bfloat16), earlier, preferred_element_type=jnp.float32)
    bound = jnp.zeros((experts, tokens), jnp.float32)
    for expert in range(experts):
        bound = jnp.where(expert_row == expert, quota_ref[expert].astype(jnp.float32), bound)
    used = jnp.where(rank < bound, weight, 0.0).astype(jnp.bfloat16)
    one = lax.broadcasted_iota(jnp.int32, (experts, experts), 0)
    two = lax.broadcasted_iota(jnp.int32, (experts, experts), 1)
    partner = jnp.where(jnp.bitwise_xor(one, 1) == two, 1.0, 0.0).astype(jnp.bfloat16)
    out_ref[:, :tokens] = used
    out_ref[:, tokens:] = jnp.dot(partner, used, preferred_element_type=jnp.float32).astype(
        jnp.bfloat16
    )


def route_table(picks, entries, coefficients, quotas):
    experts = quotas.shape[0]
    tokens = picks.shape[0]
    vmem = pl.BlockSpec(memory_space=pltpu.VMEM)
    return pl.pallas_call(
        route_table_kernel,
        out_shape=jax.ShapeDtypeStruct((experts, 2 * tokens), jnp.bfloat16),
        in_specs=[pl.BlockSpec(memory_space=pltpu.SMEM), vmem, vmem, vmem],
        out_specs=vmem,
        name="route_table",
    )(quotas, picks.T, entries.T, coefficients[None, :])


def hidden_kernel(pair_total, first_slot, place_ref, table_ref, *refs):
    block_refs = refs[: 2 * pair_total]
    gate_ref, up_ref, lhs_ref, count_ref, weigh_ref, rows_ref, coef_ref = refs[2 * pair_total :]
    tokens = block_refs[0].shape[0]

    @pl.when(pl.program_id(0) == 0)
    def _():
        core = place_ref[0]
        keep = place_ref[1].astype(jnp.float32)
        merge = place_ref[2].astype(jnp.float32)
        row = lax.broadcasted_iota(jnp.int32, (tokens, tokens), 0)
        col = lax.broadcasted_iota(jnp.int32, (tokens, tokens), 1)
        table_row = lax.broadcasted_iota(jnp.int32, table_ref.shape, 0)
        for pair in range(pair_total):
            for side in range(2):
                half = core if side == 0 else 1 - core
                start = pl.multiple_of(2 * pair * tokens + half * tokens, tokens)
                rows_ref[pl.ds(start, tokens), :] = block_refs[2 * pair + side][...]
                source = place_ref[first_slot + pair] + side
                weights = jnp.where(table_row == source, table_ref[...].astype(jnp.float32), 0.0)
                weights = jnp.sum(weights, axis=0, keepdims=True)
                own = jnp.where(row == col, weights[:, :tokens], 0.0)
                partner = jnp.where(row == col, weights[:, tokens:], 0.0)
                own = jnp.sum(own, axis=1, keepdims=True)
                partner = jnp.sum(partner, axis=1, keepdims=True)
                count = jnp.where(own > 0.0, keep, 0.0) + jnp.where(partner > 0.0, merge, 0.0)
                fixed = (2 * pair + side) * tokens
                coef_ref[0, fixed : fixed + tokens, :] = jnp.broadcast_to(count, (tokens, 128))
                coef_ref[1, fixed : fixed + tokens, :] = jnp.broadcast_to(own, (tokens, 128))

    gate = jnp.dot(rows_ref[...], gate_ref[...], preferred_element_type=jnp.float32)
    upward = jnp.dot(rows_ref[...], up_ref[...], preferred_element_type=jnp.float32)
    hidden = (gate / (1.0 + jnp.exp(-gate)) * upward).astype(jnp.bfloat16).astype(jnp.float32)
    lhs_ref[...] = hidden.T.astype(jnp.bfloat16)
    for lane in range(0, hidden.shape[1], 128):
        part = hidden[:, lane : lane + 128]
        count_ref[:, lane : lane + 128] = (part * coef_ref[0]).astype(jnp.bfloat16)
        weigh_ref[:, lane : lane + 128] = (part * coef_ref[1]).astype(jnp.bfloat16)


def hidden_parts(place, first_slot, table, blocks, w_gate, w_up, name):
    pair_total = len(blocks) // 2
    tokens, width = blocks[0].shape
    rows = len(blocks) * tokens
    hidden_width = w_gate.shape[2]
    tile = 256
    whole = pl.BlockSpec((tokens, width), lambda j, place: (0, 0))
    weights = pl.BlockSpec((None, width, tile), lambda j, place: (0, 0, j))
    out_rows = pl.BlockSpec((rows, tile), lambda j, place: (0, j))
    row_shape = jax.ShapeDtypeStruct((rows, hidden_width), jnp.bfloat16)
    return pl.pallas_call(
        functools.partial(hidden_kernel, pair_total, first_slot),
        out_shape=(
            jax.ShapeDtypeStruct((hidden_width, rows), jnp.bfloat16),
            row_shape,
            row_shape,
        ),
        grid_spec=pltpu.PrefetchScalarGridSpec(
            num_scalar_prefetch=1,
            grid=(hidden_width // tile,),
            in_specs=[
                pl.BlockSpec(table.shape, lambda j, place: (0, 0)),
                *[whole] * len(blocks),
                weights,
                weights,
            ],
            out_specs=(
                pl.BlockSpec((tile, rows), lambda j, place: (j, 0)),
                out_rows,
                out_rows,
            ),
            scratch_shapes=[
                pltpu.VMEM((rows, width), jnp.bfloat16),
                pltpu.VMEM((2, rows, 128), jnp.float32),
            ],
        ),
        compiler_params=pltpu.CompilerParams(vmem_limit_bytes=VMEM_GRANT),
        cost_estimate=pl.CostEstimate(
            flops=4 * rows * width * hidden_width,
            bytes_accessed=4 * width * hidden_width + 2 * rows * width + 6 * rows * hidden_width,
            transcendentals=rows * hidden_width,
        ),
        name=name,
    )(place, table, *blocks, w_gate, w_up)


def sums_kernel(set_total, part_total, has_base, divisor, slots, scale_ref, *refs):
    lhs = refs[:part_total]
    rest = refs[part_total:]
    rhs = [rest[part_total * index : part_total * (index + 1)] for index in range(set_total)]
    rest = rest[part_total * set_total :]
    bases = rest[:set_total] if has_base else [None] * set_total
    outs = rest[-set_total:]
    for index in range(set_total):
        total = bases[index][...] if has_base else None
        for left, right in zip(lhs, rhs[index]):
            term = jnp.dot(left[...], right[...], preferred_element_type=jnp.float32)
            total = term if total is None else total + term
        if slots is not None:
            factor = 1.0 if slots[index] is None else scale_ref[slots[index]].astype(jnp.float32)
            total = total * (factor / divisor)
        outs[index][...] = total


def sums(place, lhs, rhs_sets, bases, slots, divisor, name):
    hidden_width = lhs[0].shape[0]
    tile = 256
    rows = sum(part.shape[1] for part in lhs)
    if slots is not None:
        shape, out_spec = (1, hidden_width, hidden_width), pl.BlockSpec(
            (None, hidden_width, tile), lambda j, scale: (0, 0, j)
        )
    else:
        shape, out_spec = (hidden_width, hidden_width), pl.BlockSpec(
            (hidden_width, tile), lambda j, scale: (0, j)
        )
    operands = list(lhs)
    in_specs = [pl.BlockSpec(part.shape, lambda j, scale: (0, 0)) for part in lhs]
    for parts in rhs_sets:
        operands += parts
        in_specs += [
            pl.BlockSpec((part.shape[0], tile), lambda j, scale: (0, j)) for part in parts
        ]
    for base in bases or ():
        operands.append(base)
        in_specs.append(pl.BlockSpec((hidden_width, tile), lambda j, scale: (0, j)))
    total = len(rhs_sets)
    return pl.pallas_call(
        functools.partial(
            sums_kernel, total, len(lhs), bool(bases), float(divisor), slots
        ),
        out_shape=[jax.ShapeDtypeStruct(shape, jnp.float32)] * total,
        grid_spec=pltpu.PrefetchScalarGridSpec(
            num_scalar_prefetch=1,
            grid=(hidden_width // tile,),
            in_specs=in_specs,
            out_specs=[out_spec] * total,
        ),
        compiler_params=pltpu.CompilerParams(vmem_limit_bytes=VMEM_GRANT),
        cost_estimate=pl.CostEstimate(
            flops=2 * total * rows * hidden_width * hidden_width,
            bytes_accessed=2 * (1 + total) * rows * hidden_width
            + 4 * total * (2 if bases else 1) * hidden_width * hidden_width,
            transcendentals=0,
        ),
        name=name,
    )(place, *operands)


def gathered_shards(
    layer_inputs,
    specialist_picks,
    coefficient_lookup_entry,
    dispatch_coefficients,
    retained_specialist_flags,
    specialist_quotas,
    gating_projection,
    raising_projection,
):
    experts = retained_specialist_flags.shape[0]
    tok_rows, top_count = specialist_picks.shape
    position_ordinal = max(4, 3 * tok_rows * top_count // (4 * experts))
    me = lax.axis_index("expert")
    core = jnp.bitwise_and(me, 1)
    expert_lane = jnp.arange(experts, dtype=jnp.int32)
    keep = jnp.sum(jnp.where(expert_lane == me, retained_specialist_flags, 0))
    keep_partner = jnp.sum(
        jnp.where(expert_lane == jnp.bitwise_xor(me, 1), retained_specialist_flags, 0)
    )
    merge = keep * (1 - keep_partner)
    groups = experts // 4
    divisor = experts * position_ordinal

    def along(x):
        return lax.ppermute(x, "expert", [(i, (i + 4) % experts) for i in range(experts)])

    def back(steps):
        return jnp.bitwise_and(jnp.remainder(me + experts - 4 * steps, experts), ~1)

    firsts = [back(0)]
    for step in range(1, groups):
        firsts += [jnp.bitwise_xor(back(step - 1), 2), back(step)]
    firsts.append(jnp.bitwise_xor(back(groups - 1), 2))
    place = jnp.stack([core, keep, merge, *firsts]).astype(jnp.int32)

    def hidden(slot, blocks, name):
        return hidden_parts(
            place, 3 + slot, table, blocks, gating_projection, raising_projection, name
        )

    def other(x):
        return swapped(x, "expert", 0)

    def totals(parts, bases, name):
        return sums(
            place,
            [part[0] for part in parts],
            [[part[index] for part in parts] for index in (1, 2, 3)],
            bases,
            None,
            1,
            name,
        )

    line, side = along(layer_inputs), swapped(layer_inputs, "expert", 1)
    near = other(layer_inputs)
    table = route_table(
        specialist_picks, coefficient_lookup_entry, dispatch_coefficients, specialist_quotas
    )
    table = lax.all_to_all(table, "expert", split_axis=0, concat_axis=0, tiled=True)
    part = hidden(0, [layer_inputs, near], "hidden_0")
    waiting, bases = [], None
    for step in range(1, groups):
        part, line, side = lax.optimization_barrier((part, line, side))
        part = (*part, other(part[2]))
        next_line = along(line) if step < groups - 1 else None
        next_side = swapped(line, "expert", 1)
        blocks = [side, other(side), line, other(line)]
        new = hidden(2 * step - 1, blocks, "hidden_%d" % step)
        waiting.append(part)
        if step >= 2:
            bases = totals(waiting, bases, "totals_%d" % step)
            waiting = []
            new, bases = lax.optimization_barrier((new, bases))
        part, line, side = new, next_line, next_side
    waiting.append((*part, other(part[2])))
    bases = totals(waiting, bases, "totals_last")
    side, bases = lax.optimization_barrier((side, bases))
    last = hidden(2 * groups - 1, [side, other(side)], "hidden_last")
    arrived = other(last[2])
    gram, self_cross = sums(
        place, [last[0]], [[last[1]], [last[2]]], bases[:2], (None, 1), divisor, "own_sums"
    )
    (merge_cross,) = sums(
        place, [last[0]], [[arrived]], bases[2:], (2,), divisor, "merge_sums"
    )
    return gram, self_cross, merge_cross


def solution(mesh):
    in_specs = (
        P(("parts", "expert", "replica"), None),
        P(("parts", "expert", "replica"), None),
        P(("parts", "expert", "replica"), None),
        P(),
        P(),
        P(),
        P("expert", "replica", None),
        P("expert", "replica", None),
    )
    out_specs = (
        P(("parts", "expert"), "replica", None),
        P(("parts", "expert"), "replica", None),
        P(("parts", "expert"), "replica", None),
    )
    gather_fits = mesh.shape["replica"] == 1 and mesh.shape["expert"] == 16
    body = gathered_shards if gather_fits else shards
    return jax.shard_map(body, mesh=mesh, in_specs=in_specs, out_specs=out_specs, check_vma=False)
```

```python
import functools

import jax
import jax.numpy as jnp
from jax import lax
from jax.experimental import pallas as pl
from jax.experimental.pallas import tpu as pltpu
from jax.sharding import PartitionSpec as P


def swapped(x, axis, stride):
    return lax.ppermute(x, axis, [(i, i ^ 1 << stride) for i in range(lax.axis_size(axis))])


def hidden_rows(slot_rows, w_gate, w_up):
    gate_out = jnp.einsum("nsd,dh->nsh", slot_rows, w_gate, preferred_element_type=jnp.float32)
    upward = jnp.einsum("nsd,dh->nsh", slot_rows, w_up, preferred_element_type=jnp.float32)
    return (jax.nn.silu(gate_out) * upward).astype(jnp.bfloat16)


def weigh_rows(slot_weights, hidden):
    return (slot_weights[..., None].astype(jnp.float32) * hidden.astype(jnp.float32)).astype(
        jnp.bfloat16
    )


def dispatches_at_position(segment_ordinals, specialist_quotas, position_ordinal):
    specialist_sequence = specialist_quotas.shape[0]
    flat_ids = segment_ordinals.reshape(-1)
    route_total = flat_ids.shape[0]
    indicator_vectors = (
        flat_ids[:, None] == jnp.arange(specialist_sequence, dtype=jnp.int32)[None, :]
    ).astype(jnp.int32)
    before = jnp.cumsum(indicator_vectors, axis=0) - indicator_vectors
    route_rank = jnp.sum(before * indicator_vectors, axis=1)
    dispatch_bound = jnp.sum(indicator_vectors * specialist_quotas[None, :], axis=1)
    target = jnp.where(
        route_rank < dispatch_bound,
        flat_ids * position_ordinal + route_rank,
        specialist_sequence * position_ordinal,
    )
    empty_table = jnp.full((specialist_sequence * position_ordinal,), route_total, jnp.int32)
    return empty_table.at[target].set(jnp.arange(route_total, dtype=jnp.int32), mode="drop")


def shards(
    layer_inputs,
    specialist_picks,
    coefficient_lookup_entry,
    dispatch_coefficients,
    retained_specialist_flags,
    specialist_quotas,
    gating_projection,
    raising_projection,
):
    specialist_sequence = retained_specialist_flags.shape[0]
    replica_count = lax.axis_size("replica")
    tok_rows, top_count = specialist_picks.shape
    model_width = layer_inputs.shape[1]
    position_ordinal = max(4, 3 * tok_rows * top_count // (4 * specialist_sequence))
    own_index = lax.axis_index("expert")
    partner_index = jnp.bitwise_xor(own_index, 1)
    expert_lane = jnp.arange(specialist_sequence, dtype=jnp.int32)
    keep_own = jnp.sum(jnp.where(expert_lane == own_index, retained_specialist_flags, 0))
    keep_partner = jnp.sum(jnp.where(expert_lane == partner_index, retained_specialist_flags, 0))
    keep_flag = keep_own.astype(jnp.bfloat16)
    merge_flag = (keep_own * (1 - keep_partner)).astype(jnp.bfloat16)
    gathered_gate, gathered_up = (
        lax.all_gather(gating_projection, "replica", axis=1, tiled=True),
        lax.all_gather(raising_projection, "replica", axis=1, tiled=True),
    )
    w_gate = gathered_gate[0]
    w_up = gathered_up[0]
    dispatch_sequence = dispatches_at_position(
        specialist_picks, specialist_quotas, position_ordinal
    )
    route_total = tok_rows * top_count
    token_slot = jnp.where(
        dispatch_sequence < route_total, dispatch_sequence // top_count, tok_rows
    )
    padded_tokens = jnp.concatenate(
        [layer_inputs, jnp.zeros((1, model_width), layer_inputs.dtype)], axis=0
    )
    send_rows = padded_tokens[token_slot].reshape(
        specialist_sequence, position_ordinal, model_width
    )
    levels = dispatch_coefficients.shape[0]
    onehot_levels = (
        coefficient_lookup_entry.reshape(-1)[:, None]
        == jnp.arange(levels, dtype=jnp.int32)[None, :]
    ).astype(jnp.bfloat16)
    route_weights = jnp.dot(
        onehot_levels, dispatch_coefficients, preferred_element_type=jnp.float32
    )
    padded_weights = jnp.concatenate([route_weights, jnp.zeros((1,), jnp.float32)], axis=0)
    send_weights = (
        padded_weights[dispatch_sequence]
        .astype(jnp.bfloat16)
        .reshape(specialist_sequence, position_ordinal)
    )
    slot_rows = lax.all_to_all(send_rows, "expert", split_axis=0, concat_axis=0, tiled=True)
    slot_weights = lax.all_to_all(send_weights, "expert", split_axis=0, concat_axis=0, tiled=True)
    own_hidden = hidden_rows(slot_rows, w_gate, w_up)
    arrived, own_hidden, own_weighted = (
        slot_rows,
        own_hidden,
        weigh_rows(slot_weights, own_hidden),
    )
    partner_rows, incoming = swapped((arrived, own_weighted), "expert", 0)
    crossed = hidden_rows(partner_rows, w_gate, w_up)
    hidden_width = own_hidden.shape[-1]
    own_flat = (own_hidden * keep_flag).reshape(-1, hidden_width)
    weighted_flat = own_weighted.reshape(-1, hidden_width)
    crossed_flat = (crossed * merge_flag).reshape(-1, hidden_width)
    incoming_flat = incoming.reshape(-1, hidden_width)
    both_rows = jnp.concatenate([own_flat, crossed_flat], axis=0)
    gram_part = jnp.einsum("mi,mj->ij", both_rows, both_rows, preferred_element_type=jnp.float32)
    self_part = jnp.einsum("mi,mj->ij", own_flat, weighted_flat, preferred_element_type=jnp.float32)
    merge_part = jnp.einsum(
        "mi,mj->ij", crossed_flat, incoming_flat, preferred_element_type=jnp.float32
    )
    shared_rows = lax.psum_scatter(
        jnp.concatenate([gram_part, self_part, merge_part], axis=1),
        "replica",
        scatter_dimension=0,
        tiled=True,
    )
    slot_total = jnp.float32(replica_count * specialist_sequence * position_ordinal)
    shared_rows = shared_rows / slot_total
    gram = shared_rows[:, :hidden_width]
    self_cross = shared_rows[:, hidden_width : 2 * hidden_width]
    merge_cross = shared_rows[:, 2 * hidden_width :]
    return (gram[None], self_cross[None], merge_cross[None])


VMEM_GRANT = 16 << 20


def route_table_kernel(quota_ref, pick_ref, entry_ref, coef_ref, out_ref):
    top_count, tokens = pick_ref.shape
    experts = out_ref.shape[0]
    levels = coef_ref.shape[1]
    picks = pick_ref[...]
    entries = entry_ref[...]
    coef = coef_ref[...]
    expert_row = lax.broadcasted_iota(jnp.int32, (experts, tokens), 0)
    level_row = lax.broadcasted_iota(jnp.int32, (levels, tokens), 0)
    chosen = jnp.zeros((experts, tokens), jnp.float32)
    weight = jnp.zeros((experts, tokens), jnp.float32)
    for choice in range(top_count):
        level = jnp.where(entries[choice : choice + 1, :] == level_row, 1.0, 0.0)
        value = jnp.dot(coef, level.astype(jnp.bfloat16), preferred_element_type=jnp.float32)
        hit = picks[choice : choice + 1, :] == expert_row
        chosen = jnp.where(hit, 1.0, chosen)
        weight = jnp.where(hit, value, weight)
    row = lax.broadcasted_iota(jnp.int32, (tokens, tokens), 0)
    col = lax.broadcasted_iota(jnp.int32, (tokens, tokens), 1)
    earlier = jnp.where(row < col, 1.0, 0.0).astype(jnp.bfloat16)
    rank = jnp.dot(chosen.astype(jnp.bfloat16), earlier, preferred_element_type=jnp.float32)
    bound = jnp.zeros((experts, tokens), jnp.float32)
    for expert in range(experts):
        bound = jnp.where(expert_row == expert, quota_ref[expert].astype(jnp.float32), bound)
    used = jnp.where(rank < bound, weight, 0.0).astype(jnp.bfloat16)
    one = lax.broadcasted_iota(jnp.int32, (experts, experts), 0)
    two = lax.broadcasted_iota(jnp.int32, (experts, experts), 1)
    partner = jnp.where(jnp.bitwise_xor(one, 1) == two, 1.0, 0.0).astype(jnp.bfloat16)
    out_ref[:, :tokens] = used
    out_ref[:, tokens:] = jnp.dot(partner, used, preferred_element_type=jnp.float32).astype(
        jnp.bfloat16
    )


def route_table(picks, entries, coefficients, quotas):
    experts = quotas.shape[0]
    tokens = picks.shape[0]
    vmem = pl.BlockSpec(memory_space=pltpu.VMEM)
    return pl.pallas_call(
        route_table_kernel,
        out_shape=jax.ShapeDtypeStruct((experts, 2 * tokens), jnp.bfloat16),
        in_specs=[pl.BlockSpec(memory_space=pltpu.SMEM), vmem, vmem, vmem],
        out_specs=vmem,
        compiler_params=pltpu.CompilerParams(vmem_limit_bytes=VMEM_GRANT),
        name="route_table",
    )(quotas, picks.T, entries.T, coefficients[None, :])


def hidden_kernel(block_total, source_slot, place_ref, table_ref, *refs):
    block_refs = refs[:block_total]
    gate_ref, up_ref, lhs_ref, count_ref, weigh_ref, send_ref = refs[block_total : block_total + 6]
    rows_ref, coef_ref, arrive = refs[block_total + 6 :]
    tokens = block_refs[0].shape[0]
    hidden_width = gate_ref.shape[1]
    copies = []
    for block in range(block_total):
        target = rows_ref.at[block * tokens : (block + 1) * tokens]
        copies.append(pltpu.make_async_copy(block_refs[block], target, arrive.at[block]))
        copies[-1].start()
    keep = place_ref[1].astype(jnp.float32)
    merge = place_ref[2].astype(jnp.float32)
    row = lax.broadcasted_iota(jnp.int32, (tokens, tokens), 0)
    col = lax.broadcasted_iota(jnp.int32, (tokens, tokens), 1)
    table = table_ref[...].astype(jnp.float32)
    table_row = lax.broadcasted_iota(jnp.int32, table.shape, 0)
    for block in range(block_total):
        source = place_ref[source_slot + block]
        weights = jnp.sum(jnp.where(table_row == source, table, 0.0), axis=0, keepdims=True)
        own = jnp.where(row == col, weights[:, :tokens], 0.0)
        partner = jnp.where(row == col, weights[:, tokens:], 0.0)
        own = jnp.sum(own, axis=1, keepdims=True)
        partner = jnp.sum(partner, axis=1, keepdims=True)
        count = jnp.where(own > 0.0, keep, 0.0) + jnp.where(partner > 0.0, merge, 0.0)
        span = slice(block * tokens, (block + 1) * tokens)
        coef_ref[0, span, :] = jnp.broadcast_to(count, (tokens, 128))
        coef_ref[1, span, :] = jnp.broadcast_to(own, (tokens, 128))
    tile = 256
    for pair in range(0, block_total, 2):
        copies[pair].wait()
        copies[pair + 1].wait()
        span = slice(pair * tokens, (pair + 2) * tokens)
        rows = rows_ref[span, :]
        for start in range(0, hidden_width, tile):
            lanes = slice(start, start + tile)
            gate = jnp.dot(rows, gate_ref[:, lanes], preferred_element_type=jnp.float32)
            upward = jnp.dot(rows, up_ref[:, lanes], preferred_element_type=jnp.float32)
            hidden = (gate / (1.0 + jnp.exp(-gate)) * upward).astype(jnp.bfloat16)
            lhs_ref[lanes, span] = hidden.T
            hidden = hidden.astype(jnp.float32)
            for lane in range(0, tile, 128):
                part = hidden[:, lane : lane + 128]
                to = slice(start + lane, start + lane + 128)
                count_ref[span, to] = (part * coef_ref[0, span, :]).astype(jnp.bfloat16)
                weighed = (part * coef_ref[1, span, :]).astype(jnp.bfloat16)
                weigh_ref[span, to] = weighed
                middle = (pair + 1) * tokens
                send_ref[pair * tokens : middle, to] = weighed[tokens:]
                send_ref[middle : (pair + 2) * tokens, to] = weighed[:tokens]


def in_vmem(x):
    return pltpu.with_memory_space_constraint(x, pltpu.VMEM)


def hidden_parts(place, source_slot, table, blocks, w_gate, w_up, name):
    tokens, width = blocks[0].shape
    block_total = len(blocks)
    rows = block_total * tokens
    hidden_width = w_gate.shape[1]
    vmem = pl.BlockSpec(memory_space=pltpu.VMEM)
    outside = pl.BlockSpec(memory_space=pl.ANY)
    return pl.pallas_call(
        functools.partial(hidden_kernel, block_total, source_slot),
        out_shape=(
            pltpu.VMEM((hidden_width, rows), jnp.bfloat16),
            pltpu.VMEM((rows, hidden_width), jnp.bfloat16),
            pltpu.VMEM((rows, hidden_width), jnp.bfloat16),
            jax.ShapeDtypeStruct((rows, hidden_width), jnp.bfloat16),
        ),
        in_specs=[
            pl.BlockSpec(memory_space=pltpu.SMEM),
            vmem,
            *[outside] * block_total,
            vmem,
            vmem,
        ],
        out_specs=(vmem, vmem, vmem, vmem),
        scratch_shapes=[
            pltpu.VMEM((rows, width), jnp.bfloat16),
            pltpu.VMEM((2, rows, 128), jnp.float32),
            pltpu.SemaphoreType.DMA((block_total,)),
        ],
        compiler_params=pltpu.CompilerParams(vmem_limit_bytes=VMEM_GRANT),
        cost_estimate=pl.CostEstimate(
            flops=4 * rows * width * hidden_width,
            bytes_accessed=2 * rows * width + 2 * rows * hidden_width,
            transcendentals=rows * hidden_width,
        ),
        name=name,
    )(place, table, *blocks, in_vmem(w_gate), in_vmem(w_up))


def resident_kernel(gate_ref, up_ref, gate_out, up_out, arrive):
    copies = [
        pltpu.make_async_copy(gate_ref.at[0], gate_out, arrive.at[0]),
        pltpu.make_async_copy(up_ref.at[0], up_out, arrive.at[1]),
    ]
    for copy in copies:
        copy.start()
    for copy in copies:
        copy.wait()


def resident(w_gate, w_up):
    shape = w_gate.shape[1:]
    outside = pl.BlockSpec(memory_space=pl.ANY)
    vmem = pl.BlockSpec(memory_space=pltpu.VMEM)
    return pl.pallas_call(
        resident_kernel,
        out_shape=(pltpu.VMEM(shape, w_gate.dtype), pltpu.VMEM(shape, w_up.dtype)),
        in_specs=[outside, outside],
        out_specs=(vmem, vmem),
        scratch_shapes=[pltpu.SemaphoreType.DMA((2,))],
        compiler_params=pltpu.CompilerParams(vmem_limit_bytes=VMEM_GRANT),
        name="resident_weights",
    )(w_gate, w_up)


def totals_kernel(part_total, has_base, *refs):
    parts = [refs[4 * index : 4 * index + 4] for index in range(part_total)]
    rest = refs[4 * part_total :]
    bases = rest[:3] if has_base else None
    rest = rest[3:] if has_base else rest
    outs, landed, arrive = rest[:3], rest[3 : 3 + part_total], rest[3 + part_total]
    copies = []
    for index in range(part_total):
        copies.append(
            pltpu.make_async_copy(parts[index][3], landed[index], arrive.at[index])
        )
        copies[-1].start()
    hidden_width = outs[0].shape[1]
    tile = 256
    for which in range(3):
        if which == 2:
            for copy in copies:
                copy.wait()
        for start in range(0, hidden_width, tile):
            lanes = slice(start, start + tile)
            total = bases[which][:, lanes] if has_base else None
            for index, part in enumerate(parts):
                right = landed[index] if which == 2 else part[1 + which]
                term = jnp.dot(
                    part[0][...], right[:, lanes], preferred_element_type=jnp.float32
                )
                total = term if total is None else total + term
            outs[which][:, lanes] = total


def add_totals(parts, bases, name):
    hidden_width = parts[0][0].shape[0]
    vmem = pl.BlockSpec(memory_space=pltpu.VMEM)
    outside = pl.BlockSpec(memory_space=pl.ANY)
    operands, in_specs = [], []
    rows = 0
    for part in parts:
        rows += part[0].shape[1]
        operands += [in_vmem(part[0]), in_vmem(part[1]), in_vmem(part[2]), part[3]]
        in_specs += [vmem, vmem, vmem, outside]
    aliases = {}
    if bases is not None:
        aliases = {len(operands) + index: index for index in range(3)}
        operands += [in_vmem(base) for base in bases]
        in_specs += [vmem] * 3
    return pl.pallas_call(
        functools.partial(totals_kernel, len(parts), bases is not None),
        out_shape=[pltpu.VMEM((hidden_width, hidden_width), jnp.float32)] * 3,
        in_specs=in_specs,
        out_specs=[vmem] * 3,
        input_output_aliases=aliases,
        scratch_shapes=[
            *[pltpu.VMEM(part[3].shape, jnp.bfloat16) for part in parts],
            pltpu.SemaphoreType.DMA((len(parts),)),
        ],
        compiler_params=pltpu.CompilerParams(vmem_limit_bytes=VMEM_GRANT),
        cost_estimate=pl.CostEstimate(
            flops=6 * rows * hidden_width * hidden_width,
            bytes_accessed=2 * rows * hidden_width,
            transcendentals=0,
        ),
        name=name,
    )(*operands)


def final_kernel(set_total, slots, divisor, place_ref, lhs_ref, *refs):
    rhs, bases = refs[:set_total], refs[set_total : 2 * set_total]
    outs, done_ref, leave = refs[2 * set_total : 3 * set_total], refs[-2], refs[-1]
    hidden_width = lhs_ref.shape[0]
    tile = 256
    copies = []
    for index in range(set_total):
        factor = 1.0 if slots[index] is None else place_ref[slots[index]].astype(jnp.float32)
        factor = factor / divisor
        for start in range(0, hidden_width, tile):
            span = slice(start, start + tile)
            total = bases[index][span, :] + jnp.dot(
                lhs_ref[span, :], rhs[index][...], preferred_element_type=jnp.float32
            )
            done_ref[index, span, :] = total * factor
            copies.append(
                pltpu.make_async_copy(
                    done_ref.at[index, span],
                    outs[index].at[0, span],
                    leave.at[index, start // tile],
                )
            )
            copies[-1].start()
    for copy in copies:
        copy.wait()


def final_sums(place, lhs, rhs, bases, slots, divisor, name):
    hidden_width, rows = lhs.shape
    total = len(rhs)
    vmem = pl.BlockSpec(memory_space=pltpu.VMEM)
    outside = pl.BlockSpec(memory_space=pl.ANY)
    return pl.pallas_call(
        functools.partial(final_kernel, total, slots, float(divisor)),
        out_shape=[jax.ShapeDtypeStruct((1, hidden_width, hidden_width), jnp.float32)] * total,
        in_specs=[pl.BlockSpec(memory_space=pltpu.SMEM)] + [vmem] * (1 + 2 * total),
        out_specs=[outside] * total,
        scratch_shapes=[
            pltpu.VMEM((total, hidden_width, hidden_width), jnp.float32),
            pltpu.SemaphoreType.DMA((total, hidden_width // 256)),
        ],
        compiler_params=pltpu.CompilerParams(vmem_limit_bytes=VMEM_GRANT),
        cost_estimate=pl.CostEstimate(
            flops=2 * total * rows * hidden_width * hidden_width,
            bytes_accessed=4 * total * hidden_width * hidden_width,
            transcendentals=0,
        ),
        name=name,
    )(place, in_vmem(lhs), *rhs, *[in_vmem(base) for base in bases])


def gathered_shards(
    layer_inputs,
    specialist_picks,
    coefficient_lookup_entry,
    dispatch_coefficients,
    retained_specialist_flags,
    specialist_quotas,
    gating_projection,
    raising_projection,
):
    experts = retained_specialist_flags.shape[0]
    tok_rows, top_count = specialist_picks.shape
    position_ordinal = max(4, 3 * tok_rows * top_count // (4 * experts))
    me = lax.axis_index("expert")
    core = jnp.bitwise_and(me, 1)
    expert_lane = jnp.arange(experts, dtype=jnp.int32)
    keep = jnp.sum(jnp.where(expert_lane == me, retained_specialist_flags, 0))
    keep_partner = jnp.sum(
        jnp.where(expert_lane == jnp.bitwise_xor(me, 1), retained_specialist_flags, 0)
    )
    merge = keep * (1 - keep_partner)
    groups = experts // 4
    divisor = experts * position_ordinal

    def along(x):
        return lax.ppermute(x, "expert", [(i, (i + 4) % experts) for i in range(experts)])

    def back(steps):
        return jnp.bitwise_and(jnp.remainder(me + experts - 4 * steps, experts), ~1)

    firsts = [back(0)]
    for step in range(1, groups):
        firsts += [jnp.bitwise_xor(back(step - 1), 2), back(step)]
    firsts.append(jnp.bitwise_xor(back(groups - 1), 2))
    sources = []
    for first in firsts:
        sources += [first + core, first + 1 - core]
    place = jnp.stack([core, keep, merge, *sources]).astype(jnp.int32)
    w_gate, w_up = resident(gating_projection, raising_projection)

    def hidden(slot, blocks, name):
        return hidden_parts(place, 3 + 2 * slot, table, blocks, w_gate, w_up, name)

    def other(x):
        return swapped(x, "expert", 0)

    line, side = along(layer_inputs), swapped(layer_inputs, "expert", 1)
    near = other(layer_inputs)
    table = route_table(
        specialist_picks, coefficient_lookup_entry, dispatch_coefficients, specialist_quotas
    )
    table = lax.all_to_all(table, "expert", split_axis=0, concat_axis=0, tiled=True)
    part = hidden(0, [layer_inputs, near], "hidden_0")
    bases = None
    for step in range(1, groups):
        part, line, side = lax.optimization_barrier((part, line, side))
        part = (*part[:3], other(part[3]))
        next_line = along(line) if step < groups - 1 else None
        next_side = swapped(line, "expert", 1)
        blocks = [side, other(side), line, other(line)]
        new = hidden(2 * step - 1, blocks, "hidden_%d" % step)
        bases = add_totals([part], bases, "totals_%d" % step)
        new, bases = lax.optimization_barrier((new, bases))
        part, line, side = new, next_line, next_side
    bases = add_totals([(*part[:3], other(part[3]))], bases, "totals_last")
    side, bases = lax.optimization_barrier((side, bases))
    last = hidden(2 * groups - 1, [side, other(side)], "hidden_last")
    arrived = other(last[3])
    gram, self_cross = final_sums(
        place, last[0], [in_vmem(last[1]), in_vmem(last[2])], bases[:2], (None, 1), divisor, "own_sums"
    )
    (merge_cross,) = final_sums(
        place, last[0], [arrived], bases[2:], (2,), divisor, "merge_sums"
    )
    return gram, self_cross, merge_cross


def solution(mesh):
    in_specs = (
        P(("parts", "expert", "replica"), None),
        P(("parts", "expert", "replica"), None),
        P(("parts", "expert", "replica"), None),
        P(),
        P(),
        P(),
        P("expert", "replica", None),
        P("expert", "replica", None),
    )
    out_specs = (
        P(("parts", "expert"), "replica", None),
        P(("parts", "expert"), "replica", None),
        P(("parts", "expert"), "replica", None),
    )
    gather_fits = mesh.shape["replica"] == 1 and mesh.shape["expert"] == 16
    body = gathered_shards if gather_fits else shards
    return jax.shard_map(body, mesh=mesh, in_specs=in_specs, out_specs=out_specs, check_vma=False)
```

```python
import functools

import jax
import jax.numpy as jnp
from jax import lax
from jax.experimental import pallas as pl
from jax.experimental.pallas import tpu as pltpu
from jax.sharding import PartitionSpec as P


def swapped(x, axis, stride):
    return lax.ppermute(x, axis, [(i, i ^ 1 << stride) for i in range(lax.axis_size(axis))])


def hidden_rows(slot_rows, w_gate, w_up):
    gate_out = jnp.einsum("nsd,dh->nsh", slot_rows, w_gate, preferred_element_type=jnp.float32)
    upward = jnp.einsum("nsd,dh->nsh", slot_rows, w_up, preferred_element_type=jnp.float32)
    return (jax.nn.silu(gate_out) * upward).astype(jnp.bfloat16)


def weigh_rows(slot_weights, hidden):
    return (slot_weights[..., None].astype(jnp.float32) * hidden.astype(jnp.float32)).astype(
        jnp.bfloat16
    )


def dispatches_at_position(segment_ordinals, specialist_quotas, position_ordinal):
    specialist_sequence = specialist_quotas.shape[0]
    flat_ids = segment_ordinals.reshape(-1)
    route_total = flat_ids.shape[0]
    indicator_vectors = (
        flat_ids[:, None] == jnp.arange(specialist_sequence, dtype=jnp.int32)[None, :]
    ).astype(jnp.int32)
    before = jnp.cumsum(indicator_vectors, axis=0) - indicator_vectors
    route_rank = jnp.sum(before * indicator_vectors, axis=1)
    dispatch_bound = jnp.sum(indicator_vectors * specialist_quotas[None, :], axis=1)
    target = jnp.where(
        route_rank < dispatch_bound,
        flat_ids * position_ordinal + route_rank,
        specialist_sequence * position_ordinal,
    )
    empty_table = jnp.full((specialist_sequence * position_ordinal,), route_total, jnp.int32)
    return empty_table.at[target].set(jnp.arange(route_total, dtype=jnp.int32), mode="drop")


def shards(
    layer_inputs,
    specialist_picks,
    coefficient_lookup_entry,
    dispatch_coefficients,
    retained_specialist_flags,
    specialist_quotas,
    gating_projection,
    raising_projection,
):
    specialist_sequence = retained_specialist_flags.shape[0]
    replica_count = lax.axis_size("replica")
    tok_rows, top_count = specialist_picks.shape
    model_width = layer_inputs.shape[1]
    position_ordinal = max(4, 3 * tok_rows * top_count // (4 * specialist_sequence))
    own_index = lax.axis_index("expert")
    partner_index = jnp.bitwise_xor(own_index, 1)
    expert_lane = jnp.arange(specialist_sequence, dtype=jnp.int32)
    keep_own = jnp.sum(jnp.where(expert_lane == own_index, retained_specialist_flags, 0))
    keep_partner = jnp.sum(jnp.where(expert_lane == partner_index, retained_specialist_flags, 0))
    keep_flag = keep_own.astype(jnp.bfloat16)
    merge_flag = (keep_own * (1 - keep_partner)).astype(jnp.bfloat16)
    gathered_gate, gathered_up = (
        lax.all_gather(gating_projection, "replica", axis=1, tiled=True),
        lax.all_gather(raising_projection, "replica", axis=1, tiled=True),
    )
    w_gate = gathered_gate[0]
    w_up = gathered_up[0]
    dispatch_sequence = dispatches_at_position(
        specialist_picks, specialist_quotas, position_ordinal
    )
    route_total = tok_rows * top_count
    token_slot = jnp.where(
        dispatch_sequence < route_total, dispatch_sequence // top_count, tok_rows
    )
    padded_tokens = jnp.concatenate(
        [layer_inputs, jnp.zeros((1, model_width), layer_inputs.dtype)], axis=0
    )
    send_rows = padded_tokens[token_slot].reshape(
        specialist_sequence, position_ordinal, model_width
    )
    levels = dispatch_coefficients.shape[0]
    onehot_levels = (
        coefficient_lookup_entry.reshape(-1)[:, None]
        == jnp.arange(levels, dtype=jnp.int32)[None, :]
    ).astype(jnp.bfloat16)
    route_weights = jnp.dot(
        onehot_levels, dispatch_coefficients, preferred_element_type=jnp.float32
    )
    padded_weights = jnp.concatenate([route_weights, jnp.zeros((1,), jnp.float32)], axis=0)
    send_weights = (
        padded_weights[dispatch_sequence]
        .astype(jnp.bfloat16)
        .reshape(specialist_sequence, position_ordinal)
    )
    slot_rows = lax.all_to_all(send_rows, "expert", split_axis=0, concat_axis=0, tiled=True)
    slot_weights = lax.all_to_all(send_weights, "expert", split_axis=0, concat_axis=0, tiled=True)
    own_hidden = hidden_rows(slot_rows, w_gate, w_up)
    arrived, own_hidden, own_weighted = (
        slot_rows,
        own_hidden,
        weigh_rows(slot_weights, own_hidden),
    )
    partner_rows, incoming = swapped((arrived, own_weighted), "expert", 0)
    crossed = hidden_rows(partner_rows, w_gate, w_up)
    hidden_width = own_hidden.shape[-1]
    own_flat = (own_hidden * keep_flag).reshape(-1, hidden_width)
    weighted_flat = own_weighted.reshape(-1, hidden_width)
    crossed_flat = (crossed * merge_flag).reshape(-1, hidden_width)
    incoming_flat = incoming.reshape(-1, hidden_width)
    both_rows = jnp.concatenate([own_flat, crossed_flat], axis=0)
    gram_part = jnp.einsum("mi,mj->ij", both_rows, both_rows, preferred_element_type=jnp.float32)
    self_part = jnp.einsum("mi,mj->ij", own_flat, weighted_flat, preferred_element_type=jnp.float32)
    merge_part = jnp.einsum(
        "mi,mj->ij", crossed_flat, incoming_flat, preferred_element_type=jnp.float32
    )
    shared_rows = lax.psum_scatter(
        jnp.concatenate([gram_part, self_part, merge_part], axis=1),
        "replica",
        scatter_dimension=0,
        tiled=True,
    )
    slot_total = jnp.float32(replica_count * specialist_sequence * position_ordinal)
    shared_rows = shared_rows / slot_total
    gram = shared_rows[:, :hidden_width]
    self_cross = shared_rows[:, hidden_width : 2 * hidden_width]
    merge_cross = shared_rows[:, 2 * hidden_width :]
    return (gram[None], self_cross[None], merge_cross[None])


VMEM_GRANT = 16 << 20
SMALL_COST = pl.CostEstimate(flops=1 << 20, bytes_accessed=1 << 16, transcendentals=0)


def route_table_kernel(quota_ref, pick_ref, entry_ref, coef_ref, out_ref):
    top_count, tokens = pick_ref.shape
    experts = out_ref.shape[1]
    levels = coef_ref.shape[1]
    picks = pick_ref[...]
    entries = entry_ref[...]
    coef = coef_ref[...]
    expert_row = lax.broadcasted_iota(jnp.int32, (experts, tokens), 0)
    level_row = lax.broadcasted_iota(jnp.int32, (levels, tokens), 0)
    chosen = jnp.zeros((experts, tokens), jnp.float32)
    weight = jnp.zeros((experts, tokens), jnp.float32)
    for choice in range(top_count):
        level = jnp.where(entries[choice : choice + 1, :] == level_row, 1.0, 0.0)
        value = jnp.dot(coef, level.astype(jnp.bfloat16), preferred_element_type=jnp.float32)
        hit = picks[choice : choice + 1, :] == expert_row
        chosen = jnp.where(hit, 1.0, chosen)
        weight = jnp.where(hit, value, weight)
    row = lax.broadcasted_iota(jnp.int32, (tokens, tokens), 0)
    col = lax.broadcasted_iota(jnp.int32, (tokens, tokens), 1)
    earlier = jnp.where(row < col, 1.0, 0.0).astype(jnp.bfloat16)
    rank = jnp.dot(chosen.astype(jnp.bfloat16), earlier, preferred_element_type=jnp.float32)
    bound = jnp.zeros((experts, tokens), jnp.float32)
    for expert in range(experts):
        bound = jnp.where(expert_row == expert, quota_ref[expert].astype(jnp.float32), bound)
    used = jnp.where(rank < bound, weight, 0.0).astype(jnp.bfloat16)
    for receiver in range(experts):
        out_ref[receiver] = used


def route_table(picks, entries, coefficients, quotas):
    experts = quotas.shape[0]
    tokens = picks.shape[0]
    vmem = pl.BlockSpec(memory_space=pltpu.VMEM)
    return pl.pallas_call(
        route_table_kernel,
        out_shape=jax.ShapeDtypeStruct((experts, experts, tokens), jnp.bfloat16),
        in_specs=[pl.BlockSpec(memory_space=pltpu.SMEM), vmem, vmem, vmem],
        out_specs=vmem,
        compiler_params=pltpu.CompilerParams(vmem_limit_bytes=VMEM_GRANT),
        name="route_table",
    )(quotas, picks.T, entries.T, coefficients[None, :])


def hidden_kernel(places, table_ref, flag_ref, *refs):
    block_total = len(places)
    block_refs = refs[:block_total]
    gate_ref, up_ref, lhs_ref, count_ref, weigh_ref, send_ref = refs[block_total : block_total + 6]
    rows_ref, coef_ref, arrive = refs[block_total + 6 :]
    experts, _, tokens = table_ref.shape
    hidden_width = gate_ref.shape[2]
    copies, spans = [], []
    for block in range(block_total):
        first = spans[-1].stop if spans else 0
        spans.append(slice(first, first + block_refs[block].shape[0]))
        copies.append(
            pltpu.make_async_copy(block_refs[block], rows_ref.at[spans[block]], arrive.at[block])
        )
        copies[-1].start()
    me = lax.axis_index("expert")
    partner_index = jnp.bitwise_xor(me, 1)
    keep = flag_ref[me].astype(jnp.float32)
    merge = keep * (1.0 - flag_ref[partner_index].astype(jnp.float32))
    row = lax.broadcasted_iota(jnp.int32, (tokens, tokens), 0)
    col = lax.broadcasted_iota(jnp.int32, (tokens, tokens), 1)
    expert_row = lax.broadcasted_iota(jnp.int32, (experts, tokens), 0)
    for block, (steps, turn, offset) in enumerate(places):
        source = jnp.bitwise_xor(lax.rem(me + experts - 4 * steps, experts), turn)
        table = table_ref[source].astype(jnp.float32)
        own = jnp.sum(jnp.where(expert_row == me, table, 0.0), axis=0, keepdims=True)
        partner = jnp.sum(jnp.where(expert_row == partner_index, table, 0.0), axis=0, keepdims=True)
        own = jnp.sum(jnp.where(row == col, own, 0.0), axis=1, keepdims=True)
        partner = jnp.sum(jnp.where(row == col, partner, 0.0), axis=1, keepdims=True)
        count = jnp.where(own > 0.0, keep, 0.0) + jnp.where(partner > 0.0, merge, 0.0)
        size = spans[block].stop - spans[block].start
        part = slice(offset, offset + size)
        coef_ref[0, spans[block], :] = jnp.broadcast_to(count[part], (size, 128))
        coef_ref[1, spans[block], :] = jnp.broadcast_to(own[part], (size, 128))
    tile = 256
    groups, group = [], []
    for pair in range(0, block_total, 2):
        group.append(pair)
        if spans[pair + 1].stop - spans[group[0]].start >= 256 or pair + 2 == block_total:
            groups.append(group)
            group = []
    for group in groups:
        for pair in group:
            copies[pair].wait()
            copies[pair + 1].wait()
        span = slice(spans[group[0]].start, spans[group[-1] + 1].stop)
        rows = rows_ref[span, :]
        for start in range(0, hidden_width, tile):
            lanes = slice(start, start + tile)
            gate = jnp.dot(rows, gate_ref[0, :, lanes], preferred_element_type=jnp.float32)
            upward = jnp.dot(rows, up_ref[0, :, lanes], preferred_element_type=jnp.float32)
            hidden = (gate / (1.0 + jnp.exp(-gate)) * upward).astype(jnp.bfloat16)
            lhs_ref[lanes, span] = hidden.T
            hidden = hidden.astype(jnp.float32)
            for lane in range(0, tile, 128):
                part = hidden[:, lane : lane + 128]
                to = slice(start + lane, start + lane + 128)
                count_ref[span, to] = (part * coef_ref[0, span, :]).astype(jnp.bfloat16)
                weighed = (part * coef_ref[1, span, :]).astype(jnp.bfloat16)
                weigh_ref[span, to] = weighed
                for pair in group:
                    mine, theirs = spans[pair], spans[pair + 1]
                    base = span.start
                    send_ref[mine, to] = weighed[theirs.start - base : theirs.stop - base]
                    send_ref[theirs, to] = weighed[mine.start - base : mine.stop - base]


def in_vmem(x):
    return pltpu.with_memory_space_constraint(x, pltpu.VMEM)


def in_hbm(x):
    return pltpu.with_memory_space_constraint(x, pltpu.HBM)


def hidden_parts(places, table, flags, blocks, w_gate, w_up, name):
    width = blocks[0].shape[1]
    block_total = len(blocks)
    rows = sum(block.shape[0] for block in blocks)
    hidden_width = w_gate.shape[2]
    vmem = pl.BlockSpec(memory_space=pltpu.VMEM)
    outside = pl.BlockSpec(memory_space=pl.ANY)
    return pl.pallas_call(
        functools.partial(hidden_kernel, places),
        out_shape=(
            pltpu.VMEM((hidden_width, rows), jnp.bfloat16),
            pltpu.VMEM((rows, hidden_width), jnp.bfloat16),
            pltpu.VMEM((rows, hidden_width), jnp.bfloat16),
            jax.ShapeDtypeStruct((rows, hidden_width), jnp.bfloat16),
        ),
        in_specs=[
            vmem,
            pl.BlockSpec(memory_space=pltpu.SMEM),
            *[outside] * block_total,
            vmem,
            vmem,
        ],
        out_specs=(vmem, vmem, vmem, vmem),
        scratch_shapes=[
            pltpu.VMEM((rows, width), jnp.bfloat16),
            pltpu.VMEM((2, rows, 128), jnp.float32),
            pltpu.SemaphoreType.DMA((block_total,)),
        ],
        compiler_params=pltpu.CompilerParams(vmem_limit_bytes=VMEM_GRANT),
        cost_estimate=SMALL_COST,
        name=name,
    )(table, flags, *[in_hbm(block) for block in blocks], in_vmem(w_gate), in_vmem(w_up))


def totals_kernel(part_total, has_base, *refs):
    parts = [refs[4 * index : 4 * index + 4] for index in range(part_total)]
    rest = refs[4 * part_total :]
    bases = rest[:3] if has_base else None
    rest = rest[3:] if has_base else rest
    outs, landed, arrive = rest[:3], rest[3 : 3 + part_total], rest[3 + part_total]
    copies = []
    for index in range(part_total):
        copies.append(
            pltpu.make_async_copy(parts[index][3], landed[index], arrive.at[index])
        )
        copies[-1].start()
    hidden_width = outs[0].shape[1]
    tile = 256
    for which in range(3):
        if which == 2:
            for copy in copies:
                copy.wait()
        for start in range(0, hidden_width, tile):
            lanes = slice(start, start + tile)
            total = bases[which][:, lanes] if has_base else None
            for index, part in enumerate(parts):
                right = landed[index] if which == 2 else part[1 + which]
                term = jnp.dot(
                    part[0][...], right[:, lanes], preferred_element_type=jnp.float32
                )
                total = term if total is None else total + term
            outs[which][:, lanes] = total


def add_totals(parts, bases, name):
    hidden_width = parts[0][0].shape[0]
    vmem = pl.BlockSpec(memory_space=pltpu.VMEM)
    outside = pl.BlockSpec(memory_space=pl.ANY)
    operands, in_specs = [], []
    rows = 0
    for part in parts:
        rows += part[0].shape[1]
        operands += [in_vmem(part[0]), in_vmem(part[1]), in_vmem(part[2]), part[3]]
        in_specs += [vmem, vmem, vmem, outside]
    aliases = {}
    if bases is not None:
        aliases = {len(operands) + index: index for index in range(3)}
        operands += [in_vmem(base) for base in bases]
        in_specs += [vmem] * 3
    return pl.pallas_call(
        functools.partial(totals_kernel, len(parts), bases is not None),
        out_shape=[pltpu.VMEM((hidden_width, hidden_width), jnp.float32)] * 3,
        in_specs=in_specs,
        out_specs=[vmem] * 3,
        input_output_aliases=aliases,
        scratch_shapes=[
            *[pltpu.VMEM(part[3].shape, jnp.bfloat16) for part in parts],
            pltpu.SemaphoreType.DMA((len(parts),)),
        ],
        compiler_params=pltpu.CompilerParams(vmem_limit_bytes=VMEM_GRANT),
        cost_estimate=SMALL_COST,
        name=name,
    )(*operands)


def final_kernel(set_total, slots, divisor, flag_ref, lhs_ref, *refs):
    rhs, bases = refs[:set_total], refs[set_total : 2 * set_total]
    outs, done_ref, leave = refs[2 * set_total : 3 * set_total], refs[-2], refs[-1]
    hidden_width = lhs_ref.shape[0]
    me = lax.axis_index("expert")
    keep = flag_ref[me].astype(jnp.float32)
    keep_partner = flag_ref[jnp.bitwise_xor(me, 1)].astype(jnp.float32)
    tile = 256
    copies = []
    for index in range(set_total):
        factor = 1.0 / divisor
        if slots[index] != "gram":
            factor = factor * keep
        if slots[index] == "merge":
            factor = factor * (1.0 - keep_partner)
        for start in range(0, hidden_width, tile):
            span = slice(start, start + tile)
            total = bases[index][span, :] + jnp.dot(
                lhs_ref[span, :], rhs[index][...], preferred_element_type=jnp.float32
            )
            done_ref[index, span, :] = total * factor
            copies.append(
                pltpu.make_async_copy(
                    done_ref.at[index, span],
                    outs[index].at[0, span],
                    leave.at[index, start // tile],
                )
            )
            copies[-1].start()
    for copy in copies:
        copy.wait()


def final_sums(flags, lhs, rhs, bases, slots, divisor, name):
    hidden_width, rows = lhs.shape
    total = len(rhs)
    vmem = pl.BlockSpec(memory_space=pltpu.VMEM)
    outside = pl.BlockSpec(memory_space=pl.ANY)
    return pl.pallas_call(
        functools.partial(final_kernel, total, slots, float(divisor)),
        out_shape=[jax.ShapeDtypeStruct((1, hidden_width, hidden_width), jnp.float32)] * total,
        in_specs=[pl.BlockSpec(memory_space=pltpu.SMEM)] + [vmem] * (1 + 2 * total),
        out_specs=[outside] * total,
        scratch_shapes=[
            pltpu.VMEM((total, hidden_width, hidden_width), jnp.float32),
            pltpu.SemaphoreType.DMA((total, hidden_width // 256)),
        ],
        compiler_params=pltpu.CompilerParams(vmem_limit_bytes=VMEM_GRANT),
        cost_estimate=SMALL_COST,
        name=name,
    )(flags, in_vmem(lhs), *rhs, *[in_vmem(base) for base in bases])


def gathered_shards(
    layer_inputs,
    specialist_picks,
    coefficient_lookup_entry,
    dispatch_coefficients,
    retained_specialist_flags,
    specialist_quotas,
    gating_projection,
    raising_projection,
):
    experts = retained_specialist_flags.shape[0]
    tok_rows, top_count = specialist_picks.shape
    position_ordinal = max(4, 3 * tok_rows * top_count // (4 * experts))
    divisor = experts * position_ordinal
    half = tok_rows // 2

    def along(x):
        return lax.ppermute(x, "expert", [(i, (i + 4) % experts) for i in range(experts)])

    def across(x):
        return swapped(x, "expert", 1)

    def other(x):
        return swapped(x, "expert", 0)

    def hidden(arrivals, name):
        blocks, places = [], []
        for block, steps, turn, offset in arrivals:
            blocks += [block, other(block)]
            places += [(steps, turn, offset), (steps, turn ^ 1, offset)]
        return hidden_parts(
            places,
            table,
            retained_specialist_flags,
            blocks,
            gating_projection,
            raising_projection,
            name,
        )

    def totals(parts, bases, name):
        return add_totals([(*part[:3], other(part[3])) for part in parts], bases, name)

    tied = lax.optimization_barrier
    line_1, side_0 = along(layer_inputs), across(layer_inputs)
    table = route_table(
        specialist_picks, coefficient_lookup_entry, dispatch_coefficients, specialist_quotas
    )
    table = lax.all_to_all(table, "expert", split_axis=0, concat_axis=0, tiled=True)

    table, line_1, side_0 = tied((table, line_1, side_0))
    line_2, side_1 = along(line_1), across(line_1)
    first = [(layer_inputs, 0, 0, 0), (side_0, 0, 2, 0), (line_1, 1, 0, 0)]
    first = hidden(first, "hidden_first")

    first, line_2, side_1 = tied((first, line_2, side_1))
    upper_3, side_2 = along(line_2[:half]), across(line_2)
    lower_3 = along(line_2[half:])
    second = hidden([(side_1, 1, 2, 0), (line_2, 2, 0, 0)], "hidden_second")
    bases = totals([first], None, "totals_first")

    second, upper_3 = tied((second, upper_3))
    last_upper = across(upper_3)
    bases, lower_3, side_2 = tied((bases, lower_3, side_2))
    last_lower = across(lower_3)
    third = [(side_2, 2, 2, 0), (upper_3, 3, 0, 0), (lower_3, 3, 0, half)]
    third = hidden(third, "hidden_third")
    bases = totals([second], bases, "totals_second")
    fourth = hidden([(last_upper, 3, 2, 0)], "hidden_fourth")
    bases = totals([third, fourth], bases, "totals_third")

    bases, last_lower = tied((bases, last_lower))
    last = hidden([(last_lower, 3, 2, half)], "hidden_last")
    arrived = other(last[3])
    gram, self_cross = final_sums(
        retained_specialist_flags,
        last[0],
        [in_vmem(last[1]), in_vmem(last[2])],
        bases[:2],
        ("gram", "self"),
        divisor,
        "own_sums",
    )
    (merge_cross,) = final_sums(
        retained_specialist_flags, last[0], [arrived], bases[2:], ("merge",), divisor, "merge_sums"
    )
    return gram, self_cross, merge_cross


def solution(mesh):
    in_specs = (
        P(("parts", "expert", "replica"), None),
        P(("parts", "expert", "replica"), None),
        P(("parts", "expert", "replica"), None),
        P(),
        P(),
        P(),
        P("expert", "replica", None),
        P("expert", "replica", None),
    )
    out_specs = (
        P(("parts", "expert"), "replica", None),
        P(("parts", "expert"), "replica", None),
        P(("parts", "expert"), "replica", None),
    )
    gather_fits = mesh.shape["replica"] == 1 and mesh.shape["expert"] == 16
    body = gathered_shards if gather_fits else shards
    return jax.shard_map(body, mesh=mesh, in_specs=in_specs, out_specs=out_specs, check_vma=False)
```

```python
import functools

import jax
import jax.numpy as jnp
from jax import lax
from jax.experimental import pallas as pl
from jax.experimental.pallas import tpu as pltpu
from jax.sharding import PartitionSpec as P


def swapped(x, axis, stride):
    return lax.ppermute(x, axis, [(i, i ^ 1 << stride) for i in range(lax.axis_size(axis))])


def hidden_rows(slot_rows, w_gate, w_up):
    gate_out = jnp.einsum("nsd,dh->nsh", slot_rows, w_gate, preferred_element_type=jnp.float32)
    upward = jnp.einsum("nsd,dh->nsh", slot_rows, w_up, preferred_element_type=jnp.float32)
    return (jax.nn.silu(gate_out) * upward).astype(jnp.bfloat16)


def weigh_rows(slot_weights, hidden):
    return (slot_weights[..., None].astype(jnp.float32) * hidden.astype(jnp.float32)).astype(
        jnp.bfloat16
    )


def dispatches_at_position(segment_ordinals, specialist_quotas, position_ordinal):
    specialist_sequence = specialist_quotas.shape[0]
    flat_ids = segment_ordinals.reshape(-1)
    route_total = flat_ids.shape[0]
    indicator_vectors = (
        flat_ids[:, None] == jnp.arange(specialist_sequence, dtype=jnp.int32)[None, :]
    ).astype(jnp.int32)
    before = jnp.cumsum(indicator_vectors, axis=0) - indicator_vectors
    route_rank = jnp.sum(before * indicator_vectors, axis=1)
    dispatch_bound = jnp.sum(indicator_vectors * specialist_quotas[None, :], axis=1)
    target = jnp.where(
        route_rank < dispatch_bound,
        flat_ids * position_ordinal + route_rank,
        specialist_sequence * position_ordinal,
    )
    empty_table = jnp.full((specialist_sequence * position_ordinal,), route_total, jnp.int32)
    return empty_table.at[target].set(jnp.arange(route_total, dtype=jnp.int32), mode="drop")


def shards(
    layer_inputs,
    specialist_picks,
    coefficient_lookup_entry,
    dispatch_coefficients,
    retained_specialist_flags,
    specialist_quotas,
    gating_projection,
    raising_projection,
):
    specialist_sequence = retained_specialist_flags.shape[0]
    replica_count = lax.axis_size("replica")
    tok_rows, top_count = specialist_picks.shape
    model_width = layer_inputs.shape[1]
    position_ordinal = max(4, 3 * tok_rows * top_count // (4 * specialist_sequence))
    own_index = lax.axis_index("expert")
    partner_index = jnp.bitwise_xor(own_index, 1)
    expert_lane = jnp.arange(specialist_sequence, dtype=jnp.int32)
    keep_own = jnp.sum(jnp.where(expert_lane == own_index, retained_specialist_flags, 0))
    keep_partner = jnp.sum(jnp.where(expert_lane == partner_index, retained_specialist_flags, 0))
    keep_flag = keep_own.astype(jnp.bfloat16)
    merge_flag = (keep_own * (1 - keep_partner)).astype(jnp.bfloat16)
    gathered_gate, gathered_up = (
        lax.all_gather(gating_projection, "replica", axis=1, tiled=True),
        lax.all_gather(raising_projection, "replica", axis=1, tiled=True),
    )
    w_gate = gathered_gate[0]
    w_up = gathered_up[0]
    dispatch_sequence = dispatches_at_position(
        specialist_picks, specialist_quotas, position_ordinal
    )
    route_total = tok_rows * top_count
    token_slot = jnp.where(
        dispatch_sequence < route_total, dispatch_sequence // top_count, tok_rows
    )
    padded_tokens = jnp.concatenate(
        [layer_inputs, jnp.zeros((1, model_width), layer_inputs.dtype)], axis=0
    )
    send_rows = padded_tokens[token_slot].reshape(
        specialist_sequence, position_ordinal, model_width
    )
    levels = dispatch_coefficients.shape[0]
    onehot_levels = (
        coefficient_lookup_entry.reshape(-1)[:, None]
        == jnp.arange(levels, dtype=jnp.int32)[None, :]
    ).astype(jnp.bfloat16)
    route_weights = jnp.dot(
        onehot_levels, dispatch_coefficients, preferred_element_type=jnp.float32
    )
    padded_weights = jnp.concatenate([route_weights, jnp.zeros((1,), jnp.float32)], axis=0)
    send_weights = (
        padded_weights[dispatch_sequence]
        .astype(jnp.bfloat16)
        .reshape(specialist_sequence, position_ordinal)
    )
    slot_rows = lax.all_to_all(send_rows, "expert", split_axis=0, concat_axis=0, tiled=True)
    slot_weights = lax.all_to_all(send_weights, "expert", split_axis=0, concat_axis=0, tiled=True)
    own_hidden = hidden_rows(slot_rows, w_gate, w_up)
    arrived, own_hidden, own_weighted = (
        slot_rows,
        own_hidden,
        weigh_rows(slot_weights, own_hidden),
    )
    partner_rows, incoming = swapped((arrived, own_weighted), "expert", 0)
    crossed = hidden_rows(partner_rows, w_gate, w_up)
    hidden_width = own_hidden.shape[-1]
    own_flat = (own_hidden * keep_flag).reshape(-1, hidden_width)
    weighted_flat = own_weighted.reshape(-1, hidden_width)
    crossed_flat = (crossed * merge_flag).reshape(-1, hidden_width)
    incoming_flat = incoming.reshape(-1, hidden_width)
    both_rows = jnp.concatenate([own_flat, crossed_flat], axis=0)
    gram_part = jnp.einsum("mi,mj->ij", both_rows, both_rows, preferred_element_type=jnp.float32)
    self_part = jnp.einsum("mi,mj->ij", own_flat, weighted_flat, preferred_element_type=jnp.float32)
    merge_part = jnp.einsum(
        "mi,mj->ij", crossed_flat, incoming_flat, preferred_element_type=jnp.float32
    )
    shared_rows = lax.psum_scatter(
        jnp.concatenate([gram_part, self_part, merge_part], axis=1),
        "replica",
        scatter_dimension=0,
        tiled=True,
    )
    slot_total = jnp.float32(replica_count * specialist_sequence * position_ordinal)
    shared_rows = shared_rows / slot_total
    gram = shared_rows[:, :hidden_width]
    self_cross = shared_rows[:, hidden_width : 2 * hidden_width]
    merge_cross = shared_rows[:, 2 * hidden_width :]
    return (gram[None], self_cross[None], merge_cross[None])


def kernel_cost(flops):
    return pl.CostEstimate(flops=flops, bytes_accessed=1 << 16, transcendentals=0)


def in_hbm(x):
    return pltpu.with_memory_space_constraint(x, pltpu.HBM)


def route_table_kernel(
    quota_ref, pick_in, entry_in, coef_ref, out_ref, pick_ref, entry_ref, arrive
):
    copies = [
        pltpu.make_async_copy(pick_in, pick_ref, arrive.at[0]),
        pltpu.make_async_copy(entry_in, entry_ref, arrive.at[1]),
    ]
    for copy in copies:
        copy.start()
    for copy in copies:
        copy.wait()
    top_count, tokens = pick_ref.shape
    experts = out_ref.shape[0]
    levels = coef_ref.shape[1]
    picks = pick_ref[...]
    entries = entry_ref[...]
    coef = coef_ref[...]
    expert_row = lax.broadcasted_iota(jnp.int32, (experts, tokens), 0)
    level_row = lax.broadcasted_iota(jnp.int32, (levels, tokens), 0)
    chosen = jnp.zeros((experts, tokens), jnp.float32)
    weight = jnp.zeros((experts, tokens), jnp.float32)
    for choice in range(top_count):
        level = jnp.where(entries[choice : choice + 1, :] == level_row, 1.0, 0.0)
        value = jnp.dot(coef, level.astype(jnp.bfloat16), preferred_element_type=jnp.float32)
        hit = picks[choice : choice + 1, :] == expert_row
        chosen = jnp.where(hit, 1.0, chosen)
        weight = jnp.where(hit, value, weight)
    row = lax.broadcasted_iota(jnp.int32, (tokens, tokens), 0)
    col = lax.broadcasted_iota(jnp.int32, (tokens, tokens), 1)
    earlier = jnp.where(row < col, 1.0, 0.0).astype(jnp.bfloat16)
    rank = jnp.dot(chosen.astype(jnp.bfloat16), earlier, preferred_element_type=jnp.float32)
    bound = jnp.zeros((experts, tokens), jnp.float32)
    for expert in range(experts):
        bound = jnp.where(expert_row == expert, quota_ref[expert].astype(jnp.float32), bound)
    used = jnp.where(rank < bound, weight, 0.0).astype(jnp.bfloat16)
    for receiver in range(experts):
        out_ref[receiver, 0:1, :] = used[receiver : receiver + 1]
        out_ref[receiver, 1:2, :] = used[receiver ^ 1 : (receiver ^ 1) + 1]


def route_table(picks, entries, coefficients, quotas):
    experts = quotas.shape[0]
    tokens = picks.shape[0]
    vmem = pl.BlockSpec(memory_space=pltpu.VMEM)
    outside = pl.BlockSpec(memory_space=pl.ANY)
    return pl.pallas_call(
        route_table_kernel,
        out_shape=jax.ShapeDtypeStruct((experts, 2, tokens), jnp.bfloat16),
        in_specs=[pl.BlockSpec(memory_space=pltpu.SMEM), outside, outside, vmem],
        out_specs=vmem,
        scratch_shapes=[
            pltpu.VMEM(picks.shape[::-1], jnp.int32),
            pltpu.VMEM(entries.shape[::-1], jnp.int32),
            pltpu.SemaphoreType.DMA((2,)),
        ],
        compiler_params=pltpu.CompilerParams(vmem_limit_bytes=4 << 20),
        name="route_table",
    )(quotas, in_hbm(picks.T), in_hbm(entries.T), coefficients[None, :])


def stage_kernel(places, with_part, with_base, *refs):
    taken = iter(refs)

    def take(count):
        return [next(taken) for _ in range(count)]

    table_ref, flag_ref = take(2)
    blocks = take(len(places))
    weights = take(2)
    part = take(4) if with_part else None
    bases = take(3) if with_base else None
    hidden_outs = take(4)
    sums = take(3) if with_part else None
    scratch = take(2)
    if with_part:
        totals_body([part], bases, sums)
    hidden_body(places, table_ref, flag_ref, blocks, *weights, *hidden_outs, *scratch)


def hidden_body(
    places,
    table_ref,
    flag_ref,
    block_refs,
    gate_ref,
    up_ref,
    lhs_ref,
    count_ref,
    weigh_ref,
    send_ref,
    rows_ref,
    coef_ref,
):
    block_total = len(places)
    experts, _, tokens = table_ref.shape
    hidden_width = gate_ref.shape[2]
    spans = []
    for block in range(block_total):
        first = spans[-1].stop if spans else 0
        spans.append(slice(first, first + block_refs[block].shape[0]))
        rows_ref[spans[block], :] = block_refs[block][...]
    me = lax.axis_index("expert")
    keep = flag_ref[me].astype(jnp.float32)
    merge = keep * (1.0 - flag_ref[jnp.bitwise_xor(me, 1)].astype(jnp.float32))
    row = lax.broadcasted_iota(jnp.int32, (tokens, tokens), 0)
    col = lax.broadcasted_iota(jnp.int32, (tokens, tokens), 1)
    for block, (steps, turn, offset) in enumerate(places):
        source = jnp.bitwise_xor(lax.rem(me + experts - 4 * steps, experts), turn)
        table = table_ref[source].astype(jnp.float32)
        own = jnp.sum(jnp.where(row == col, table[0:1], 0.0), axis=1, keepdims=True)
        partner = jnp.sum(jnp.where(row == col, table[1:2], 0.0), axis=1, keepdims=True)
        count = jnp.where(own > 0.0, keep, 0.0) + jnp.where(partner > 0.0, merge, 0.0)
        size = spans[block].stop - spans[block].start
        part = slice(offset, offset + size)
        coef_ref[0, spans[block], :] = jnp.broadcast_to(count[part], (size, 128))
        coef_ref[1, spans[block], :] = jnp.broadcast_to(own[part], (size, 128))
    tile = 256
    groups, group = [], []
    for pair in range(0, block_total, 2):
        group.append(pair)
        if spans[pair + 1].stop - spans[group[0]].start >= 256 or pair + 2 == block_total:
            groups.append(group)
            group = []
    for group in groups:
        span = slice(spans[group[0]].start, spans[group[-1] + 1].stop)
        rows = rows_ref[span, :]
        for start in range(0, hidden_width, tile):
            lanes = slice(start, start + tile)
            gate = jnp.dot(rows, gate_ref[0, :, lanes], preferred_element_type=jnp.float32)
            upward = jnp.dot(rows, up_ref[0, :, lanes], preferred_element_type=jnp.float32)
            hidden = (gate / (1.0 + jnp.exp(-gate)) * upward).astype(jnp.bfloat16)
            lhs_ref[lanes, span] = hidden.T
            hidden = hidden.astype(jnp.float32)
            for lane in range(0, tile, 128):
                part = hidden[:, lane : lane + 128]
                to = slice(start + lane, start + lane + 128)
                count_ref[span, to] = (part * coef_ref[0, span, :]).astype(jnp.bfloat16)
                weighed = (part * coef_ref[1, span, :]).astype(jnp.bfloat16)
                weigh_ref[span, to] = weighed
                for pair in group:
                    mine, theirs = spans[pair], spans[pair + 1]
                    base = span.start
                    send_ref[mine, to] = weighed[theirs.start - base : theirs.stop - base]
                    send_ref[theirs, to] = weighed[mine.start - base : mine.stop - base]


def in_vmem(x):
    return pltpu.with_memory_space_constraint(x, pltpu.VMEM)


def run_stage(places, table, flags, blocks, w_gate, w_up, part, bases, name):
    width = blocks[0].shape[1]
    rows = sum(block.shape[0] for block in blocks)
    hidden_width = w_gate.shape[2]
    vmem = pl.BlockSpec(memory_space=pltpu.VMEM)
    operands = [in_vmem(table), flags, *map(in_vmem, blocks), in_vmem(w_gate), in_vmem(w_up)]
    out_shape = [
        pltpu.VMEM((hidden_width, rows), jnp.bfloat16),
        pltpu.VMEM((rows, hidden_width), jnp.bfloat16),
        pltpu.VMEM((rows, hidden_width), jnp.bfloat16),
        jax.ShapeDtypeStruct((rows, hidden_width), jnp.bfloat16),
    ]
    aliases = {}
    if part is not None:
        operands += map(in_vmem, part)
        out_shape += [pltpu.VMEM((hidden_width, hidden_width), jnp.float32)] * 3
    if bases is not None:
        aliases = {len(operands) + index: 4 + index for index in range(3)}
        operands += map(in_vmem, bases)
    in_specs = [vmem] * len(operands)
    in_specs[1] = pl.BlockSpec(memory_space=pltpu.SMEM)
    outs = pl.pallas_call(
        functools.partial(stage_kernel, places, part is not None, bases is not None),
        out_shape=out_shape,
        in_specs=in_specs,
        out_specs=[vmem] * len(out_shape),
        input_output_aliases=aliases,
        scratch_shapes=[
            pltpu.VMEM((rows, width), jnp.bfloat16),
            pltpu.VMEM((2, rows, 128), jnp.float32),
        ],
        compiler_params=pltpu.CompilerParams(vmem_limit_bytes=10 << 20),
        cost_estimate=kernel_cost(4 * rows * width * hidden_width),
        name=name,
    )(*operands)
    return tuple(outs[:4]), tuple(outs[4:])


def totals_body(parts, bases, outs):
    hidden_width = outs[0].shape[1]
    tile = 256
    for which in range(3):
        for start in range(0, hidden_width, tile):
            lanes = slice(start, start + tile)
            total = None if bases is None else bases[which][:, lanes]
            for part in parts:
                term = jnp.dot(
                    part[0][...], part[1 + which][:, lanes], preferred_element_type=jnp.float32
                )
                total = term if total is None else total + term
            outs[which][:, lanes] = total


def totals_kernel(*refs):
    totals_body([refs[:4]], refs[4:7], refs[7:])


def add_totals(part, bases, name):
    hidden_width, rows = part[0].shape
    vmem = pl.BlockSpec(memory_space=pltpu.VMEM)
    return pl.pallas_call(
        totals_kernel,
        out_shape=[pltpu.VMEM((hidden_width, hidden_width), jnp.float32)] * 3,
        in_specs=[vmem] * 7,
        out_specs=[vmem] * 3,
        input_output_aliases={4: 0, 5: 1, 6: 2},
        compiler_params=pltpu.CompilerParams(vmem_limit_bytes=6 << 20),
        cost_estimate=kernel_cost(6 * rows * hidden_width * hidden_width),
        name=name,
    )(*map(in_vmem, part), *map(in_vmem, bases))


def pick_kernel(even_ref, odd_ref, out_ref):
    core = jnp.bitwise_and(lax.axis_index("expert"), 1)

    @pl.when(core == 0)
    def _():
        out_ref[...] = even_ref[...]

    @pl.when(core == 1)
    def _():
        out_ref[...] = odd_ref[...]


def pick_by_core(even, odd):
    vmem = pl.BlockSpec(memory_space=pltpu.VMEM)
    return pl.pallas_call(
        pick_kernel,
        out_shape=pltpu.VMEM(even.shape, even.dtype),
        in_specs=[vmem, vmem],
        out_specs=vmem,
        compiler_params=pltpu.CompilerParams(vmem_limit_bytes=4 << 20),
        name="pick_by_core",
    )(in_vmem(even), in_vmem(odd))


def final_kernel(set_total, slots, divisor, flag_ref, lhs_ref, *refs):
    rhs, bases = refs[:set_total], refs[set_total : 2 * set_total]
    outs, done_ref, leave = refs[2 * set_total : 3 * set_total], refs[-2], refs[-1]
    hidden_width = lhs_ref.shape[0]
    me = lax.axis_index("expert")
    keep = flag_ref[me].astype(jnp.float32)
    keep_partner = flag_ref[jnp.bitwise_xor(me, 1)].astype(jnp.float32)
    tile = 256
    copies = []
    for index in range(set_total):
        factor = 1.0 / divisor
        if slots[index] != "gram":
            factor = factor * keep
        if slots[index] == "merge":
            factor = factor * (1.0 - keep_partner)
        for start in range(0, hidden_width, tile):
            span = slice(start, start + tile)
            total = bases[index][span, :] + jnp.dot(
                lhs_ref[span, :], rhs[index][...], preferred_element_type=jnp.float32
            )
            done_ref[index, span, :] = total * factor
            copies.append(
                pltpu.make_async_copy(
                    done_ref.at[index, span],
                    outs[index].at[0, span],
                    leave.at[index, start // tile],
                )
            )
            copies[-1].start()
    for copy in copies:
        copy.wait()


def final_sums(flags, lhs, rhs, bases, slots, divisor, name):
    hidden_width, rows = lhs.shape
    total = len(rhs)
    vmem = pl.BlockSpec(memory_space=pltpu.VMEM)
    outside = pl.BlockSpec(memory_space=pl.ANY)
    return pl.pallas_call(
        functools.partial(final_kernel, total, slots, float(divisor)),
        out_shape=[jax.ShapeDtypeStruct((1, hidden_width, hidden_width), jnp.float32)] * total,
        in_specs=[pl.BlockSpec(memory_space=pltpu.SMEM)] + [vmem] * (1 + 2 * total),
        out_specs=[outside] * total,
        scratch_shapes=[
            pltpu.VMEM((total, hidden_width, hidden_width), jnp.float32),
            pltpu.SemaphoreType.DMA((total, hidden_width // 256)),
        ],
        compiler_params=pltpu.CompilerParams(vmem_limit_bytes=8 << 20),
        cost_estimate=kernel_cost(1 << 20),
        name=name,
    )(flags, in_vmem(lhs), *rhs, *[in_vmem(base) for base in bases])


def gathered_shards(
    layer_inputs,
    specialist_picks,
    coefficient_lookup_entry,
    dispatch_coefficients,
    retained_specialist_flags,
    specialist_quotas,
    gating_projection,
    raising_projection,
):
    experts = retained_specialist_flags.shape[0]
    tok_rows, top_count = specialist_picks.shape
    position_ordinal = max(4, 3 * tok_rows * top_count // (4 * experts))
    divisor = experts * position_ordinal

    def along(x):
        return lax.ppermute(x, "expert", [(i, (i + 4) % experts) for i in range(experts)])

    def across(x):
        return swapped(x, "expert", 1)

    def other(x):
        return swapped(x, "expert", 0)

    def stage(arrivals, part, bases, name):
        blocks, places = [], []
        for block, steps, turn, offset in arrivals:
            blocks += [block, other(block)]
            places += [(steps, turn, offset), (steps, turn ^ 1, offset)]
        return run_stage(
            places,
            table,
            retained_specialist_flags,
            blocks,
            gating_projection,
            raising_projection,
            None if part is None else (*part[:3], other(part[3])),
            bases,
            name,
        )

    tied = lax.optimization_barrier
    line_1, side_0 = along(layer_inputs), across(layer_inputs)
    table = route_table(
        specialist_picks, coefficient_lookup_entry, dispatch_coefficients, specialist_quotas
    )
    table = lax.all_to_all(table, "expert", split_axis=0, concat_axis=0, tiled=True)

    table, line_1, side_0 = tied((table, line_1, side_0))
    line_2, side_1 = along(line_1), across(line_1)
    first = [(layer_inputs, 0, 0, 0), (side_0, 0, 2, 0), (line_1, 1, 0, 0)]
    first, _ = stage(first, None, None, "stage_first")

    first, line_2, side_1 = tied((first, line_2, side_1))
    line_3, side_2 = along(line_2), across(line_2)
    second = [(side_1, 1, 2, 0), (line_2, 2, 0, 0)]
    second, bases = stage(second, first, None, "stage_second")

    second, bases, line_3, side_2 = tied((second, bases, line_3, side_2))
    fourth = [(i, i ^ 2) if i % 2 == 0 else (i, (i + 4) % experts) for i in range(experts)]
    side_3 = lax.ppermute(pick_by_core(line_3, side_2), "expert", fourth)
    third = [(side_2, 2, 2, 0), (line_3, 3, 0, 0)]
    third, bases = stage(third, second, bases, "stage_third")

    third, bases, side_3 = tied((third, bases, side_3))
    bases = add_totals((*third[:3], other(third[3])), bases, "totals_third")
    last, _ = stage([(side_3, 3, 2, 0)], None, None, "stage_last")
    arrived = other(last[3])
    gram, self_cross = final_sums(
        retained_specialist_flags,
        last[0],
        [in_vmem(last[1]), in_vmem(last[2])],
        bases[:2],
        ("gram", "self"),
        divisor,
        "own_sums",
    )
    (merge_cross,) = final_sums(
        retained_specialist_flags, last[0], [arrived], bases[2:], ("merge",), divisor, "merge_sums"
    )
    return gram, self_cross, merge_cross


def solution(mesh):
    in_specs = (
        P(("parts", "expert", "replica"), None),
        P(("parts", "expert", "replica"), None),
        P(("parts", "expert", "replica"), None),
        P(),
        P(),
        P(),
        P("expert", "replica", None),
        P("expert", "replica", None),
    )
    out_specs = (
        P(("parts", "expert"), "replica", None),
        P(("parts", "expert"), "replica", None),
        P(("parts", "expert"), "replica", None),
    )
    gather_fits = mesh.shape["replica"] == 1 and mesh.shape["expert"] == 16
    body = gathered_shards if gather_fits else shards
    return jax.shard_map(body, mesh=mesh, in_specs=in_specs, out_specs=out_specs, check_vma=False)
```

```python
import functools

import jax
import jax.numpy as jnp
from jax import lax
from jax.experimental import pallas as pl
from jax.experimental.pallas import tpu as pltpu
from jax.sharding import PartitionSpec as P


def swapped(x, axis, stride):
    return lax.ppermute(x, axis, [(i, i ^ 1 << stride) for i in range(lax.axis_size(axis))])


def hidden_rows(slot_rows, w_gate, w_up):
    gate_out = jnp.einsum("nsd,dh->nsh", slot_rows, w_gate, preferred_element_type=jnp.float32)
    upward = jnp.einsum("nsd,dh->nsh", slot_rows, w_up, preferred_element_type=jnp.float32)
    return (jax.nn.silu(gate_out) * upward).astype(jnp.bfloat16)


def weigh_rows(slot_weights, hidden):
    return (slot_weights[..., None].astype(jnp.float32) * hidden.astype(jnp.float32)).astype(
        jnp.bfloat16
    )


def dispatches_at_position(segment_ordinals, specialist_quotas, position_ordinal):
    specialist_sequence = specialist_quotas.shape[0]
    flat_ids = segment_ordinals.reshape(-1)
    route_total = flat_ids.shape[0]
    indicator_vectors = (
        flat_ids[:, None] == jnp.arange(specialist_sequence, dtype=jnp.int32)[None, :]
    ).astype(jnp.int32)
    before = jnp.cumsum(indicator_vectors, axis=0) - indicator_vectors
    route_rank = jnp.sum(before * indicator_vectors, axis=1)
    dispatch_bound = jnp.sum(indicator_vectors * specialist_quotas[None, :], axis=1)
    target = jnp.where(
        route_rank < dispatch_bound,
        flat_ids * position_ordinal + route_rank,
        specialist_sequence * position_ordinal,
    )
    empty_table = jnp.full((specialist_sequence * position_ordinal,), route_total, jnp.int32)
    return empty_table.at[target].set(jnp.arange(route_total, dtype=jnp.int32), mode="drop")


def shards(
    layer_inputs,
    specialist_picks,
    coefficient_lookup_entry,
    dispatch_coefficients,
    retained_specialist_flags,
    specialist_quotas,
    gating_projection,
    raising_projection,
):
    specialist_sequence = retained_specialist_flags.shape[0]
    replica_count = lax.axis_size("replica")
    tok_rows, top_count = specialist_picks.shape
    model_width = layer_inputs.shape[1]
    position_ordinal = max(4, 3 * tok_rows * top_count // (4 * specialist_sequence))
    own_index = lax.axis_index("expert")
    partner_index = jnp.bitwise_xor(own_index, 1)
    expert_lane = jnp.arange(specialist_sequence, dtype=jnp.int32)
    keep_own = jnp.sum(jnp.where(expert_lane == own_index, retained_specialist_flags, 0))
    keep_partner = jnp.sum(jnp.where(expert_lane == partner_index, retained_specialist_flags, 0))
    keep_flag = keep_own.astype(jnp.bfloat16)
    merge_flag = (keep_own * (1 - keep_partner)).astype(jnp.bfloat16)
    gathered_gate, gathered_up = (
        lax.all_gather(gating_projection, "replica", axis=1, tiled=True),
        lax.all_gather(raising_projection, "replica", axis=1, tiled=True),
    )
    w_gate = gathered_gate[0]
    w_up = gathered_up[0]
    dispatch_sequence = dispatches_at_position(
        specialist_picks, specialist_quotas, position_ordinal
    )
    route_total = tok_rows * top_count
    token_slot = jnp.where(
        dispatch_sequence < route_total, dispatch_sequence // top_count, tok_rows
    )
    padded_tokens = jnp.concatenate(
        [layer_inputs, jnp.zeros((1, model_width), layer_inputs.dtype)], axis=0
    )
    send_rows = padded_tokens[token_slot].reshape(
        specialist_sequence, position_ordinal, model_width
    )
    levels = dispatch_coefficients.shape[0]
    onehot_levels = (
        coefficient_lookup_entry.reshape(-1)[:, None]
        == jnp.arange(levels, dtype=jnp.int32)[None, :]
    ).astype(jnp.bfloat16)
    route_weights = jnp.dot(
        onehot_levels, dispatch_coefficients, preferred_element_type=jnp.float32
    )
    padded_weights = jnp.concatenate([route_weights, jnp.zeros((1,), jnp.float32)], axis=0)
    send_weights = (
        padded_weights[dispatch_sequence]
        .astype(jnp.bfloat16)
        .reshape(specialist_sequence, position_ordinal)
    )
    slot_rows = lax.all_to_all(send_rows, "expert", split_axis=0, concat_axis=0, tiled=True)
    slot_weights = lax.all_to_all(send_weights, "expert", split_axis=0, concat_axis=0, tiled=True)
    own_hidden = hidden_rows(slot_rows, w_gate, w_up)
    arrived, own_hidden, own_weighted = (
        slot_rows,
        own_hidden,
        weigh_rows(slot_weights, own_hidden),
    )
    partner_rows, incoming = swapped((arrived, own_weighted), "expert", 0)
    crossed = hidden_rows(partner_rows, w_gate, w_up)
    hidden_width = own_hidden.shape[-1]
    own_flat = (own_hidden * keep_flag).reshape(-1, hidden_width)
    weighted_flat = own_weighted.reshape(-1, hidden_width)
    crossed_flat = (crossed * merge_flag).reshape(-1, hidden_width)
    incoming_flat = incoming.reshape(-1, hidden_width)
    both_rows = jnp.concatenate([own_flat, crossed_flat], axis=0)
    gram_part = jnp.einsum("mi,mj->ij", both_rows, both_rows, preferred_element_type=jnp.float32)
    self_part = jnp.einsum("mi,mj->ij", own_flat, weighted_flat, preferred_element_type=jnp.float32)
    merge_part = jnp.einsum(
        "mi,mj->ij", crossed_flat, incoming_flat, preferred_element_type=jnp.float32
    )
    shared_rows = lax.psum_scatter(
        jnp.concatenate([gram_part, self_part, merge_part], axis=1),
        "replica",
        scatter_dimension=0,
        tiled=True,
    )
    slot_total = jnp.float32(replica_count * specialist_sequence * position_ordinal)
    shared_rows = shared_rows / slot_total
    gram = shared_rows[:, :hidden_width]
    self_cross = shared_rows[:, hidden_width : 2 * hidden_width]
    merge_cross = shared_rows[:, 2 * hidden_width :]
    return (gram[None], self_cross[None], merge_cross[None])


def kernel_cost(flops):
    return pl.CostEstimate(flops=flops, bytes_accessed=1 << 16, transcendentals=0)


def in_hbm(x):
    return pltpu.with_memory_space_constraint(x, pltpu.HBM)


def route_table_kernel(
    quota_ref, pick_in, entry_in, coef_in, out_ref, pick_ref, entry_ref, coef_ref, arrive
):
    copies = [
        pltpu.make_async_copy(pick_in, pick_ref, arrive.at[0]),
        pltpu.make_async_copy(entry_in, entry_ref, arrive.at[1]),
        pltpu.make_async_copy(coef_in, coef_ref, arrive.at[2]),
    ]
    for copy in copies:
        copy.start()
    for copy in copies:
        copy.wait()
    top_count, tokens = pick_ref.shape
    experts = out_ref.shape[0]
    levels = coef_ref.shape[0]
    picks = pick_ref[...]
    entries = entry_ref[...]
    coef = coef_ref[...].reshape(1, levels)
    expert_row = lax.broadcasted_iota(jnp.int32, (experts, tokens), 0)
    level_row = lax.broadcasted_iota(jnp.int32, (levels, tokens), 0)
    chosen = jnp.zeros((experts, tokens), jnp.float32)
    weight = jnp.zeros((experts, tokens), jnp.float32)
    for choice in range(top_count):
        level = jnp.where(entries[choice : choice + 1, :] == level_row, 1.0, 0.0)
        value = jnp.dot(coef, level.astype(jnp.bfloat16), preferred_element_type=jnp.float32)
        hit = picks[choice : choice + 1, :] == expert_row
        chosen = jnp.where(hit, 1.0, chosen)
        weight = jnp.where(hit, value, weight)
    row = lax.broadcasted_iota(jnp.int32, (tokens, tokens), 0)
    col = lax.broadcasted_iota(jnp.int32, (tokens, tokens), 1)
    earlier = jnp.where(row < col, 1.0, 0.0).astype(jnp.bfloat16)
    rank = jnp.dot(chosen.astype(jnp.bfloat16), earlier, preferred_element_type=jnp.float32)
    bound = jnp.zeros((experts, tokens), jnp.float32)
    for expert in range(experts):
        bound = jnp.where(expert_row == expert, quota_ref[expert].astype(jnp.float32), bound)
    used = jnp.where(rank < bound, weight, 0.0).astype(jnp.bfloat16)
    for receiver in range(experts):
        out_ref[receiver, 0:1, :] = used[receiver : receiver + 1]
        out_ref[receiver, 1:2, :] = used[receiver ^ 1 : (receiver ^ 1) + 1]


def route_table(picks, entries, coefficients, quotas):
    experts = quotas.shape[0]
    tokens = picks.shape[0]
    vmem = pl.BlockSpec(memory_space=pltpu.VMEM)
    outside = pl.BlockSpec(memory_space=pl.ANY)
    return pl.pallas_call(
        route_table_kernel,
        out_shape=jax.ShapeDtypeStruct((experts, 2, tokens), jnp.bfloat16),
        in_specs=[pl.BlockSpec(memory_space=pltpu.SMEM), outside, outside, outside],
        out_specs=vmem,
        scratch_shapes=[
            pltpu.VMEM(picks.shape[::-1], jnp.int32),
            pltpu.VMEM(entries.shape[::-1], jnp.int32),
            pltpu.VMEM(coefficients.shape, coefficients.dtype),
            pltpu.SemaphoreType.DMA((3,)),
        ],
        compiler_params=pltpu.CompilerParams(vmem_limit_bytes=4 << 20),
        name="route_table",
    )(quotas, in_hbm(picks.T), in_hbm(entries.T), in_hbm(coefficients))


def ring_neighbour(me, experts, steps, turn):
    rows = experts // 4
    row, side, core = me // 4, jnp.bitwise_and(me // 2, 1), jnp.bitwise_and(me, 1)
    position = jnp.where(side == 0, row, 2 * rows - 1 - row)
    position = lax.rem(position + steps + 2 * rows, 2 * rows)
    far = position >= rows
    row = jnp.where(far, 2 * rows - 1 - position, position)
    return 4 * row + jnp.where(far, 2, 0) + jnp.bitwise_xor(core, turn)


def ring_pairs(experts, directions):
    rows = experts // 4
    chips = [2 * row for row in range(rows)] + [2 * row + 1 for row in reversed(range(rows))]
    return [
        (2 * chip + core, 2 * chips[(position + directions[core]) % len(chips)] + core)
        for position, chip in enumerate(chips)
        for core in range(2)
    ]


def stage_kernel(places, before, after, with_base, *refs):
    taken = iter(refs)

    def take(count):
        return [next(taken) for _ in range(count)]

    table_ref, flag_ref = take(2)
    blocks = take(len(places))
    weights = take(2)
    part = take(4) if before else None
    bases = take(3) if with_base else [None] * 3
    hidden_outs = take(4)
    sums = take(3) if before or after else [None] * 3
    scratch = take(2)
    for which in before:
        add_product(sums[which], bases[which], part[0], part[1 + which])
    hidden_body(places, table_ref, flag_ref, blocks, *weights, *hidden_outs, *scratch)
    for which in after:
        base = sums[which] if which in before else bases[which]
        add_product(sums[which], base, hidden_outs[0], hidden_outs[1 + which])


def add_product(out_ref, base_ref, lhs_ref, rhs_ref):
    hidden_width = out_ref.shape[1]
    tile = 256
    for start in range(0, hidden_width, tile):
        lanes = slice(start, start + tile)
        total = jnp.dot(lhs_ref[...], rhs_ref[:, lanes], preferred_element_type=jnp.float32)
        out_ref[:, lanes] = total if base_ref is None else base_ref[:, lanes] + total


def hidden_body(
    places,
    table_ref,
    flag_ref,
    block_refs,
    gate_ref,
    up_ref,
    lhs_ref,
    count_ref,
    weigh_ref,
    send_ref,
    rows_ref,
    coef_ref,
):
    block_total = len(places)
    experts, _, tokens = table_ref.shape
    hidden_width = gate_ref.shape[2]
    spans = []
    for block in range(block_total):
        first = spans[-1].stop if spans else 0
        spans.append(slice(first, first + block_refs[block].shape[0]))
        rows_ref[spans[block], :] = block_refs[block][...]
    me = lax.axis_index("expert")
    keep = flag_ref[me].astype(jnp.float32)
    merge = keep * (1.0 - flag_ref[jnp.bitwise_xor(me, 1)].astype(jnp.float32))
    row = lax.broadcasted_iota(jnp.int32, (tokens, tokens), 0)
    col = lax.broadcasted_iota(jnp.int32, (tokens, tokens), 1)
    for block, (steps, turn, offset) in enumerate(places):
        source = ring_neighbour(me, experts, steps, turn)
        table = table_ref[source].astype(jnp.float32)
        own = jnp.sum(jnp.where(row == col, table[0:1], 0.0), axis=1, keepdims=True)
        partner = jnp.sum(jnp.where(row == col, table[1:2], 0.0), axis=1, keepdims=True)
        count = jnp.where(own > 0.0, keep, 0.0) + jnp.where(partner > 0.0, merge, 0.0)
        size = spans[block].stop - spans[block].start
        part = slice(offset, offset + size)
        coef_ref[0, spans[block], :] = jnp.broadcast_to(count[part], (size, 128))
        coef_ref[1, spans[block], :] = jnp.broadcast_to(own[part], (size, 128))
    tile = 256
    units = [(0,)] if block_total == 1 else [(i, i + 1) for i in range(0, block_total, 2)]
    groups, group = [], []
    for unit in units:
        group.append(unit)
        if spans[unit[-1]].stop - spans[group[0][0]].start >= 256 or unit == units[-1]:
            groups.append(group)
            group = []
    for group in groups:
        span = slice(spans[group[0][0]].start, spans[group[-1][-1]].stop)
        rows = rows_ref[span, :]
        for start in range(0, hidden_width, tile):
            lanes = slice(start, start + tile)
            gate = jnp.dot(rows, gate_ref[0, :, lanes], preferred_element_type=jnp.float32)
            upward = jnp.dot(rows, up_ref[0, :, lanes], preferred_element_type=jnp.float32)
            hidden = (gate / (1.0 + jnp.exp(-gate)) * upward).astype(jnp.bfloat16)
            lhs_ref[lanes, span] = hidden.T
            hidden = hidden.astype(jnp.float32)
            for lane in range(0, tile, 128):
                part = hidden[:, lane : lane + 128]
                to = slice(start + lane, start + lane + 128)
                count_ref[span, to] = (part * coef_ref[0, span, :]).astype(jnp.bfloat16)
                weighed = (part * coef_ref[1, span, :]).astype(jnp.bfloat16)
                weigh_ref[span, to] = weighed
                for unit in group:
                    for block, source in zip(unit, unit[::-1]):
                        base = span.start
                        piece = slice(spans[source].start - base, spans[source].stop - base)
                        send_ref[spans[block], to] = weighed[piece]


def in_vmem(x):
    return pltpu.with_memory_space_constraint(x, pltpu.VMEM)


def run_stage(places, table, flags, blocks, w_gate, w_up, part, bases, before, after, name):
    width = blocks[0].shape[1]
    rows = sum(block.shape[0] for block in blocks)
    hidden_width = w_gate.shape[2]
    vmem = pl.BlockSpec(memory_space=pltpu.VMEM)
    operands = [in_vmem(table), flags, *map(in_vmem, blocks), in_vmem(w_gate), in_vmem(w_up)]
    out_shape = [
        pltpu.VMEM((hidden_width, rows), jnp.bfloat16),
        pltpu.VMEM((rows, hidden_width), jnp.bfloat16),
        pltpu.VMEM((rows, hidden_width), jnp.bfloat16),
        jax.ShapeDtypeStruct((rows, hidden_width), jnp.bfloat16),
    ]
    aliases = {}
    if before:
        operands += map(in_vmem, part)
    if before or after:
        out_shape += [pltpu.VMEM((hidden_width, hidden_width), jnp.float32)] * 3
    if bases is not None:
        aliases = {len(operands) + index: 4 + index for index in range(3)}
        operands += map(in_vmem, bases)
    in_specs = [vmem] * len(operands)
    in_specs[1] = pl.BlockSpec(memory_space=pltpu.SMEM)
    outs = pl.pallas_call(
        functools.partial(stage_kernel, places, before, after, bases is not None),
        out_shape=out_shape,
        in_specs=in_specs,
        out_specs=[vmem] * len(out_shape),
        input_output_aliases=aliases,
        scratch_shapes=[
            pltpu.VMEM((rows, width), jnp.bfloat16),
            pltpu.VMEM((2, rows, 128), jnp.float32),
        ],
        compiler_params=pltpu.CompilerParams(vmem_limit_bytes=10 << 20),
        cost_estimate=kernel_cost(4 * rows * width * hidden_width),
        name=name,
    )(*operands)
    return tuple(outs[:4]), tuple(outs[4:])


def pick_kernel(even_ref, odd_ref, out_ref):
    core = jnp.bitwise_and(lax.axis_index("expert"), 1)

    @pl.when(core == 0)
    def _():
        out_ref[...] = even_ref[...]

    @pl.when(core == 1)
    def _():
        out_ref[...] = odd_ref[...]


def pick_by_core(even, odd):
    vmem = pl.BlockSpec(memory_space=pltpu.VMEM)
    return pl.pallas_call(
        pick_kernel,
        out_shape=pltpu.VMEM(even.shape, even.dtype),
        in_specs=[vmem, vmem],
        out_specs=vmem,
        compiler_params=pltpu.CompilerParams(vmem_limit_bytes=4 << 20),
        name="pick_by_core",
    )(in_vmem(even), in_vmem(odd))


def final_kernel(kinds, part_total, divisor, flag_ref, *refs):
    set_total = len(kinds)
    lhs, rest = refs[:part_total], refs[part_total:]
    rhs = [rest[part_total * index : part_total * (index + 1)] for index in range(set_total)]
    rest = rest[part_total * set_total :]
    bases, outs = rest[:set_total], rest[set_total : 2 * set_total]
    done_ref, leave = rest[2 * set_total :]
    hidden_width = lhs[0].shape[0]
    me = lax.axis_index("expert")
    keep = flag_ref[me].astype(jnp.float32)
    keep_partner = flag_ref[jnp.bitwise_xor(me, 1)].astype(jnp.float32)
    tile = 256
    copies = []
    for index in range(set_total):
        factor = 1.0 / divisor
        if kinds[index] != "gram":
            factor = factor * keep
        if kinds[index] == "merge":
            factor = factor * (1.0 - keep_partner)
        for start in range(0, hidden_width, tile):
            span = slice(start, start + tile)
            total = bases[index][span, :]
            for left, right in zip(lhs, rhs[index]):
                total = total + jnp.dot(
                    left[span, :], right[...], preferred_element_type=jnp.float32
                )
            done_ref[index, span, :] = total * factor
            copies.append(
                pltpu.make_async_copy(
                    done_ref.at[index, span],
                    outs[index].at[0, span],
                    leave.at[index, start // tile],
                )
            )
            copies[-1].start()
    for copy in copies:
        copy.wait()


def final_sums(flags, lhs, rhs, bases, kinds, divisor, name):
    hidden_width = lhs[0].shape[0]
    total = len(rhs)
    vmem = pl.BlockSpec(memory_space=pltpu.VMEM)
    outside = pl.BlockSpec(memory_space=pl.ANY)
    operands = [*lhs]
    for parts in rhs:
        operands += parts
    operands += bases
    return pl.pallas_call(
        functools.partial(final_kernel, kinds, len(lhs), float(divisor)),
        out_shape=[jax.ShapeDtypeStruct((1, hidden_width, hidden_width), jnp.float32)] * total,
        in_specs=[pl.BlockSpec(memory_space=pltpu.SMEM)] + [vmem] * len(operands),
        out_specs=[outside] * total,
        scratch_shapes=[
            pltpu.VMEM((total, hidden_width, hidden_width), jnp.float32),
            pltpu.SemaphoreType.DMA((total, hidden_width // 256)),
        ],
        compiler_params=pltpu.CompilerParams(vmem_limit_bytes=8 << 20),
        cost_estimate=kernel_cost(1 << 20),
        name=name,
    )(flags, *map(in_vmem, operands))


def gathered_shards(
    layer_inputs,
    specialist_picks,
    coefficient_lookup_entry,
    dispatch_coefficients,
    retained_specialist_flags,
    specialist_quotas,
    gating_projection,
    raising_projection,
):
    experts = retained_specialist_flags.shape[0]
    tok_rows, top_count = specialist_picks.shape
    position_ordinal = max(4, 3 * tok_rows * top_count // (4 * experts))
    divisor = experts * position_ordinal

    def onward(x):
        return lax.ppermute(x, "expert", ring_pairs(experts, (1, 1)))

    def backward(x):
        return lax.ppermute(x, "expert", ring_pairs(experts, (-1, -1)))

    def other(x):
        return swapped(x, "expert", 0)

    def stage(arrivals, part, bases, before, after, name):
        blocks, places = [], []
        for block, steps, turn, offset in arrivals:
            blocks.append(block)
            places.append((steps, turn, offset))
            if len(arrivals) > 1:
                blocks.append(other(block))
                places.append((steps, turn ^ 1, offset))
        return run_stage(
            places,
            table,
            retained_specialist_flags,
            blocks,
            gating_projection,
            raising_projection,
            None if part is None else (*part[:3], other(part[3])),
            bases,
            before,
            after,
            name,
        )

    tied = lax.optimization_barrier
    left_1, right_1 = onward(layer_inputs), backward(layer_inputs)
    table = route_table(
        specialist_picks, coefficient_lookup_entry, dispatch_coefficients, specialist_quotas
    )
    table = lax.all_to_all(table, "expert", split_axis=0, concat_axis=0, tiled=True)

    table, left_1, right_1 = tied((table, left_1, right_1))
    left_2, right_2 = onward(left_1), backward(right_1)
    first = [(layer_inputs, 0, 0, 0), (left_1, -1, 0, 0), (right_1, 1, 0, 0)]
    first, _ = stage(first, None, None, (), (), "stage_first")

    first, left_2, right_2 = tied((first, left_2, right_2))
    left_3, right_3 = onward(left_2), backward(right_2)
    second = [(left_2, -2, 0, 0), (right_2, 2, 0, 0)]
    second, bases = stage(second, first, None, (0, 1, 2), (0, 1), "stage_second")

    second, bases, left_3, right_3 = tied((second, bases, left_3, right_3))
    far = lax.ppermute(pick_by_core(left_3, right_3), "expert", ring_pairs(experts, (1, -1)))
    third = [(left_3, -3, 0, 0), (right_3, 3, 0, 0)]
    third, bases = stage(third, second, bases, (2,), (0, 1), "stage_third")

    third, bases, far = tied((third, bases, far))
    near_far = other(far)
    mine, _ = stage([(far, 4, 0, 0)], None, None, (), (), "stage_mine")
    mine, near_far = tied((mine, near_far))
    theirs, _ = stage([(near_far, 4, 1, 0)], None, None, (), (), "stage_theirs")
    last = [mine, theirs]
    gram, self_cross = final_sums(
        retained_specialist_flags,
        [part[0] for part in last],
        [[part[1] for part in last], [part[2] for part in last]],
        bases[:2],
        ("gram", "self"),
        divisor,
        "own_sums",
    )
    (merge_cross,) = final_sums(
        retained_specialist_flags,
        [third[0], mine[0], theirs[0]],
        [[other(third[3]), other(theirs[3]), other(mine[3])]],
        bases[2:],
        ("merge",),
        divisor,
        "merge_sums",
    )
    return gram, self_cross, merge_cross


def solution(mesh):
    in_specs = (
        P(("parts", "expert", "replica"), None),
        P(("parts", "expert", "replica"), None),
        P(("parts", "expert", "replica"), None),
        P(),
        P(),
        P(),
        P("expert", "replica", None),
        P("expert", "replica", None),
    )
    out_specs = (
        P(("parts", "expert"), "replica", None),
        P(("parts", "expert"), "replica", None),
        P(("parts", "expert"), "replica", None),
    )
    gather_fits = mesh.shape["replica"] == 1 and mesh.shape["expert"] == 16
    body = gathered_shards if gather_fits else shards
    return jax.shard_map(body, mesh=mesh, in_specs=in_specs, out_specs=out_specs, check_vma=False)
```

```python
import functools

import jax
import jax.numpy as jnp
from jax import lax
from jax.experimental import pallas as pl
from jax.experimental.pallas import tpu as pltpu
from jax.sharding import PartitionSpec as P


def swapped(x, axis, stride):
    return lax.ppermute(x, axis, [(i, i ^ 1 << stride) for i in range(lax.axis_size(axis))])


def hidden_rows(slot_rows, w_gate, w_up):
    gate_out = jnp.einsum("nsd,dh->nsh", slot_rows, w_gate, preferred_element_type=jnp.float32)
    upward = jnp.einsum("nsd,dh->nsh", slot_rows, w_up, preferred_element_type=jnp.float32)
    return (jax.nn.silu(gate_out) * upward).astype(jnp.bfloat16)


def weigh_rows(slot_weights, hidden):
    return (slot_weights[..., None].astype(jnp.float32) * hidden.astype(jnp.float32)).astype(
        jnp.bfloat16
    )


def dispatches_at_position(segment_ordinals, specialist_quotas, position_ordinal):
    specialist_sequence = specialist_quotas.shape[0]
    flat_ids = segment_ordinals.reshape(-1)
    route_total = flat_ids.shape[0]
    indicator_vectors = (
        flat_ids[:, None] == jnp.arange(specialist_sequence, dtype=jnp.int32)[None, :]
    ).astype(jnp.int32)
    before = jnp.cumsum(indicator_vectors, axis=0) - indicator_vectors
    route_rank = jnp.sum(before * indicator_vectors, axis=1)
    dispatch_bound = jnp.sum(indicator_vectors * specialist_quotas[None, :], axis=1)
    target = jnp.where(
        route_rank < dispatch_bound,
        flat_ids * position_ordinal + route_rank,
        specialist_sequence * position_ordinal,
    )
    empty_table = jnp.full((specialist_sequence * position_ordinal,), route_total, jnp.int32)
    return empty_table.at[target].set(jnp.arange(route_total, dtype=jnp.int32), mode="drop")


def shards(
    layer_inputs,
    specialist_picks,
    coefficient_lookup_entry,
    dispatch_coefficients,
    retained_specialist_flags,
    specialist_quotas,
    gating_projection,
    raising_projection,
):
    specialist_sequence = retained_specialist_flags.shape[0]
    replica_count = lax.axis_size("replica")
    tok_rows, top_count = specialist_picks.shape
    model_width = layer_inputs.shape[1]
    position_ordinal = max(4, 3 * tok_rows * top_count // (4 * specialist_sequence))
    own_index = lax.axis_index("expert")
    partner_index = jnp.bitwise_xor(own_index, 1)
    expert_lane = jnp.arange(specialist_sequence, dtype=jnp.int32)
    keep_own = jnp.sum(jnp.where(expert_lane == own_index, retained_specialist_flags, 0))
    keep_partner = jnp.sum(jnp.where(expert_lane == partner_index, retained_specialist_flags, 0))
    keep_flag = keep_own.astype(jnp.bfloat16)
    merge_flag = (keep_own * (1 - keep_partner)).astype(jnp.bfloat16)
    gathered_gate, gathered_up = (
        lax.all_gather(gating_projection, "replica", axis=1, tiled=True),
        lax.all_gather(raising_projection, "replica", axis=1, tiled=True),
    )
    w_gate = gathered_gate[0]
    w_up = gathered_up[0]
    dispatch_sequence = dispatches_at_position(
        specialist_picks, specialist_quotas, position_ordinal
    )
    route_total = tok_rows * top_count
    token_slot = jnp.where(
        dispatch_sequence < route_total, dispatch_sequence // top_count, tok_rows
    )
    padded_tokens = jnp.concatenate(
        [layer_inputs, jnp.zeros((1, model_width), layer_inputs.dtype)], axis=0
    )
    send_rows = padded_tokens[token_slot].reshape(
        specialist_sequence, position_ordinal, model_width
    )
    levels = dispatch_coefficients.shape[0]
    onehot_levels = (
        coefficient_lookup_entry.reshape(-1)[:, None]
        == jnp.arange(levels, dtype=jnp.int32)[None, :]
    ).astype(jnp.bfloat16)
    route_weights = jnp.dot(
        onehot_levels, dispatch_coefficients, preferred_element_type=jnp.float32
    )
    padded_weights = jnp.concatenate([route_weights, jnp.zeros((1,), jnp.float32)], axis=0)
    send_weights = (
        padded_weights[dispatch_sequence]
        .astype(jnp.bfloat16)
        .reshape(specialist_sequence, position_ordinal)
    )
    slot_rows = lax.all_to_all(send_rows, "expert", split_axis=0, concat_axis=0, tiled=True)
    slot_weights = lax.all_to_all(send_weights, "expert", split_axis=0, concat_axis=0, tiled=True)
    own_hidden = hidden_rows(slot_rows, w_gate, w_up)
    arrived, own_hidden, own_weighted = (
        slot_rows,
        own_hidden,
        weigh_rows(slot_weights, own_hidden),
    )
    partner_rows, incoming = swapped((arrived, own_weighted), "expert", 0)
    crossed = hidden_rows(partner_rows, w_gate, w_up)
    hidden_width = own_hidden.shape[-1]
    own_flat = (own_hidden * keep_flag).reshape(-1, hidden_width)
    weighted_flat = own_weighted.reshape(-1, hidden_width)
    crossed_flat = (crossed * merge_flag).reshape(-1, hidden_width)
    incoming_flat = incoming.reshape(-1, hidden_width)
    both_rows = jnp.concatenate([own_flat, crossed_flat], axis=0)
    gram_part = jnp.einsum("mi,mj->ij", both_rows, both_rows, preferred_element_type=jnp.float32)
    self_part = jnp.einsum("mi,mj->ij", own_flat, weighted_flat, preferred_element_type=jnp.float32)
    merge_part = jnp.einsum(
        "mi,mj->ij", crossed_flat, incoming_flat, preferred_element_type=jnp.float32
    )
    shared_rows = lax.psum_scatter(
        jnp.concatenate([gram_part, self_part, merge_part], axis=1),
        "replica",
        scatter_dimension=0,
        tiled=True,
    )
    slot_total = jnp.float32(replica_count * specialist_sequence * position_ordinal)
    shared_rows = shared_rows / slot_total
    gram = shared_rows[:, :hidden_width]
    self_cross = shared_rows[:, hidden_width : 2 * hidden_width]
    merge_cross = shared_rows[:, 2 * hidden_width :]
    return (gram[None], self_cross[None], merge_cross[None])


def kernel_cost(flops):
    return pl.CostEstimate(flops=flops, bytes_accessed=1 << 16, transcendentals=0)


def in_hbm(x):
    return pltpu.with_memory_space_constraint(x, pltpu.HBM)


def route_table_kernel(
    quota_ref, pick_in, entry_in, coef_in, out_ref, pick_ref, entry_ref, coef_ref, arrive
):
    copies = [
        pltpu.make_async_copy(pick_in, pick_ref, arrive.at[0]),
        pltpu.make_async_copy(entry_in, entry_ref, arrive.at[1]),
        pltpu.make_async_copy(coef_in, coef_ref, arrive.at[2]),
    ]
    for copy in copies:
        copy.start()
    for copy in copies:
        copy.wait()
    top_count, tokens = pick_ref.shape
    experts = out_ref.shape[0]
    levels = coef_ref.shape[0]
    picks = pick_ref[...]
    entries = entry_ref[...]
    coef = coef_ref[...].reshape(1, levels)
    expert_row = lax.broadcasted_iota(jnp.int32, (experts, tokens), 0)
    level_row = lax.broadcasted_iota(jnp.int32, (levels, tokens), 0)
    chosen = jnp.zeros((experts, tokens), jnp.float32)
    weight = jnp.zeros((experts, tokens), jnp.float32)
    for choice in range(top_count):
        level = jnp.where(entries[choice : choice + 1, :] == level_row, 1.0, 0.0)
        value = jnp.dot(coef, level.astype(jnp.bfloat16), preferred_element_type=jnp.float32)
        hit = picks[choice : choice + 1, :] == expert_row
        chosen = jnp.where(hit, 1.0, chosen)
        weight = jnp.where(hit, value, weight)
    row = lax.broadcasted_iota(jnp.int32, (tokens, tokens), 0)
    col = lax.broadcasted_iota(jnp.int32, (tokens, tokens), 1)
    earlier = jnp.where(row < col, 1.0, 0.0).astype(jnp.bfloat16)
    rank = jnp.dot(chosen.astype(jnp.bfloat16), earlier, preferred_element_type=jnp.float32)
    bound = jnp.zeros((experts, tokens), jnp.float32)
    for expert in range(experts):
        bound = jnp.where(expert_row == expert, quota_ref[expert].astype(jnp.float32), bound)
    used = jnp.where(rank < bound, weight, 0.0).astype(jnp.bfloat16)
    for receiver in range(experts):
        out_ref[receiver, 0:1, :] = used[receiver : receiver + 1]
        out_ref[receiver, 1:2, :] = used[receiver ^ 1 : (receiver ^ 1) + 1]


def route_table(picks, entries, coefficients, quotas):
    experts = quotas.shape[0]
    tokens = picks.shape[0]
    vmem = pl.BlockSpec(memory_space=pltpu.VMEM)
    outside = pl.BlockSpec(memory_space=pl.ANY)
    return pl.pallas_call(
        route_table_kernel,
        out_shape=jax.ShapeDtypeStruct((experts, 2, tokens), jnp.bfloat16),
        in_specs=[pl.BlockSpec(memory_space=pltpu.SMEM), outside, outside, outside],
        out_specs=vmem,
        scratch_shapes=[
            pltpu.VMEM(picks.shape[::-1], jnp.int32),
            pltpu.VMEM(entries.shape[::-1], jnp.int32),
            pltpu.VMEM(coefficients.shape, coefficients.dtype),
            pltpu.SemaphoreType.DMA((3,)),
        ],
        compiler_params=pltpu.CompilerParams(vmem_limit_bytes=4 << 20),
        cost_estimate=kernel_cost(1 << 34),
        name="route_table",
    )(quotas, in_hbm(picks.T), in_hbm(entries.T), in_hbm(coefficients))


def ring_neighbour(me, experts, steps, turn):
    rows = experts // 4
    row, side, core = me // 4, jnp.bitwise_and(me // 2, 1), jnp.bitwise_and(me, 1)
    position = jnp.where(side == 0, row, 2 * rows - 1 - row)
    position = lax.rem(position + steps + 2 * rows, 2 * rows)
    far = position >= rows
    row = jnp.where(far, 2 * rows - 1 - position, position)
    return 4 * row + jnp.where(far, 2, 0) + jnp.bitwise_xor(core, turn)


def ring_pairs(experts, directions):
    rows = experts // 4
    chips = [2 * row for row in range(rows)] + [2 * row + 1 for row in reversed(range(rows))]
    return [
        (2 * chip + core, 2 * chips[(position + directions[core]) % len(chips)] + core)
        for position, chip in enumerate(chips)
        for core in range(2)
    ]


def stage_kernel(places, before, after, with_base, rows_at, *refs):
    taken = iter(refs)

    def take(count):
        return [next(taken) for _ in range(count)]

    table_ref, flag_ref = take(2)
    blocks = take(len(places))
    weights = take(2)
    part = take(4) if before else None
    sum_total = max((*before, *after), default=-1) + 1
    bases = take(sum_total) if with_base else [None] * 3
    take(4 if rows_at else 0)
    hidden_outs = take(4)
    sums = take(sum_total)
    scratch = take(2)
    for which in before:
        add_product(sums[which], bases[which], [(part[0], part[1 + which])])
    hidden_body(places, rows_at, table_ref, flag_ref, blocks, *weights, *hidden_outs, *scratch)
    for which in after:
        base = sums[which] if which in before else bases[which]
        add_product(sums[which], base, [(hidden_outs[0], hidden_outs[1 + which])])


def add_product(out_ref, base_ref, pairs):
    hidden_width = out_ref.shape[1]
    tile = 256
    for start in range(0, hidden_width, tile):
        lanes = slice(start, start + tile)
        total = None if base_ref is None else base_ref[:, lanes]
        for lhs_ref, rhs_ref in pairs:
            term = jnp.dot(lhs_ref[...], rhs_ref[:, lanes], preferred_element_type=jnp.float32)
            total = term if total is None else total + term
        out_ref[:, lanes] = total


def hidden_body(
    places,
    rows_at,
    table_ref,
    flag_ref,
    block_refs,
    gate_ref,
    up_ref,
    lhs_ref,
    count_ref,
    weigh_ref,
    send_ref,
    rows_ref,
    coef_ref,
):
    block_total = len(places)
    experts, _, tokens = table_ref.shape
    hidden_width = gate_ref.shape[2]
    spans = []
    for block in range(block_total):
        first = spans[-1].stop if spans else 0
        spans.append(slice(first, first + block_refs[block].shape[0]))
        rows_ref[spans[block], :] = block_refs[block][...]
    me = lax.axis_index("expert")
    keep = flag_ref[me].astype(jnp.float32)
    merge = keep * (1.0 - flag_ref[jnp.bitwise_xor(me, 1)].astype(jnp.float32))
    row = lax.broadcasted_iota(jnp.int32, (tokens, tokens), 0)
    col = lax.broadcasted_iota(jnp.int32, (tokens, tokens), 1)
    for block, (steps, turn, offset) in enumerate(places):
        source = ring_neighbour(me, experts, steps, turn)
        table = table_ref[source].astype(jnp.float32)
        own = jnp.sum(jnp.where(row == col, table[0:1], 0.0), axis=1, keepdims=True)
        partner = jnp.sum(jnp.where(row == col, table[1:2], 0.0), axis=1, keepdims=True)
        count = jnp.where(own > 0.0, keep, 0.0) + jnp.where(partner > 0.0, merge, 0.0)
        size = spans[block].stop - spans[block].start
        part = slice(offset, offset + size)
        coef_ref[0, spans[block], :] = jnp.broadcast_to(count[part], (size, 128))
        coef_ref[1, spans[block], :] = jnp.broadcast_to(own[part], (size, 128))
    tile = 256
    units = [(0,)] if block_total == 1 else [(i, i + 1) for i in range(0, block_total, 2)]
    groups, group = [], []
    for unit in units:
        group.append(unit)
        if spans[unit[-1]].stop - spans[group[0][0]].start >= 256 or unit == units[-1]:
            groups.append(group)
            group = []
    for group in groups:
        span = slice(spans[group[0][0]].start, spans[group[-1][-1]].stop)
        rows = rows_ref[span, :]
        for start in range(0, hidden_width, tile):
            lanes = slice(start, start + tile)
            gate = jnp.dot(rows, gate_ref[0, :, lanes], preferred_element_type=jnp.float32)
            upward = jnp.dot(rows, up_ref[0, :, lanes], preferred_element_type=jnp.float32)
            hidden = (gate / (1.0 + jnp.exp(-gate)) * upward).astype(jnp.bfloat16)
            out_span = slice(span.start + rows_at, span.stop + rows_at)
            lhs_ref[lanes, out_span] = hidden.T
            hidden = hidden.astype(jnp.float32)
            for lane in range(0, tile, 128):
                part = hidden[:, lane : lane + 128]
                to = slice(start + lane, start + lane + 128)
                count_ref[out_span, to] = (part * coef_ref[0, span, :]).astype(jnp.bfloat16)
                weighed = (part * coef_ref[1, span, :]).astype(jnp.bfloat16)
                weigh_ref[out_span, to] = weighed
                if block_total == 1:
                    send_at = send_ref.shape[0] - span.stop - rows_at
                    send_ref[send_at : send_at + span.stop, to] = weighed
                    continue
                for unit in group:
                    for block, source in zip(unit, unit[::-1]):
                        base = span.start
                        piece = slice(spans[source].start - base, spans[source].stop - base)
                        send_ref[spans[block], to] = weighed[piece]


def in_vmem(x):
    return pltpu.with_memory_space_constraint(x, pltpu.VMEM)


def run_stage(
    places, table, flags, blocks, w_gate, w_up, part, bases, before, after, name, room=1, filled=None
):
    width = blocks[0].shape[1]
    rows = sum(block.shape[0] for block in blocks)
    hidden_width = w_gate.shape[2]
    vmem = pl.BlockSpec(memory_space=pltpu.VMEM)
    operands = [in_vmem(table), flags, *map(in_vmem, blocks), in_vmem(w_gate), in_vmem(w_up)]
    out_shape = [
        pltpu.VMEM((hidden_width, room * rows), jnp.bfloat16),
        pltpu.VMEM((room * rows, hidden_width), jnp.bfloat16),
        pltpu.VMEM((room * rows, hidden_width), jnp.bfloat16),
        pltpu.VMEM((room * rows, hidden_width), jnp.bfloat16),
    ]
    aliases = {}
    if before:
        operands += map(in_vmem, part)
    sum_total = max((*before, *after), default=-1) + 1
    out_shape += [pltpu.VMEM((hidden_width, hidden_width), jnp.float32)] * sum_total
    if bases is not None:
        aliases = {len(operands) + index: 4 + index for index in range(sum_total)}
        operands += map(in_vmem, bases)
    if filled is not None:
        aliases |= {len(operands) + index: index for index in range(4)}
        operands += map(in_vmem, filled)
    in_specs = [vmem] * len(operands)
    in_specs[1] = pl.BlockSpec(memory_space=pltpu.SMEM)
    outs = pl.pallas_call(
        functools.partial(
            stage_kernel, places, before, after, bases is not None, 0 if filled is None else rows
        ),
        out_shape=out_shape,
        in_specs=in_specs,
        out_specs=[vmem] * len(out_shape),
        input_output_aliases=aliases,
        scratch_shapes=[
            pltpu.VMEM((rows, width), jnp.bfloat16),
            pltpu.VMEM((2, rows, 128), jnp.float32),
        ],
        compiler_params=pltpu.CompilerParams(vmem_limit_bytes=10 << 20),
        cost_estimate=kernel_cost(4 * rows * width * hidden_width),
        name=name,
    )(*operands)
    return tuple(outs[:4]), tuple(outs[4:])


def pick_kernel(even_ref, odd_ref, out_ref):
    core = jnp.bitwise_and(lax.axis_index("expert"), 1)

    @pl.when(core == 0)
    def _():
        out_ref[...] = even_ref[...]

    @pl.when(core == 1)
    def _():
        out_ref[...] = odd_ref[...]


def pick_by_core(even, odd):
    vmem = pl.BlockSpec(memory_space=pltpu.VMEM)
    return pl.pallas_call(
        pick_kernel,
        out_shape=pltpu.VMEM(even.shape, even.dtype),
        in_specs=[vmem, vmem],
        out_specs=vmem,
        compiler_params=pltpu.CompilerParams(vmem_limit_bytes=4 << 20),
        name="pick_by_core",
    )(in_vmem(even), in_vmem(odd))


def final_kernel(kinds, part_total, late_total, divisor, flag_ref, *refs):
    set_total = len(kinds)
    if late_total:
        late, refs = refs[: 2 * late_total + 1], refs[2 * late_total + 1 :]
        late_out = refs[-3]
        refs = refs[:-3] + refs[-2:]
    lhs, rest = refs[:part_total], refs[part_total:]
    rhs = [rest[part_total * index : part_total * (index + 1)] for index in range(set_total)]
    rest = rest[part_total * set_total :]
    bases, outs = rest[:set_total], rest[set_total : 2 * set_total]
    done_ref, leave = rest[2 * set_total :]
    hidden_width = lhs[0].shape[0]
    me = lax.axis_index("expert")
    keep = flag_ref[me].astype(jnp.float32)
    keep_partner = flag_ref[jnp.bitwise_xor(me, 1)].astype(jnp.float32)
    tile = 256
    copies = []
    for index in range(set_total):
        factor = 1.0 / divisor
        if kinds[index] != "gram":
            factor = factor * keep
        if kinds[index] == "merge":
            factor = factor * (1.0 - keep_partner)
        for start in range(0, hidden_width, tile):
            span = slice(start, start + tile)
            total = bases[index][span, :]
            for left, right in zip(lhs, rhs[index]):
                total = total + jnp.dot(
                    left[span, :], right[...], preferred_element_type=jnp.float32
                )
            done_ref[index, span, :] = total * factor
            copies.append(
                pltpu.make_async_copy(
                    done_ref.at[index, span],
                    outs[index].at[0, span],
                    leave.at[index, start // tile],
                )
            )
            copies[-1].start()
    if late_total:
        pairs = [(late[index], late[late_total + index]) for index in range(late_total)]
        add_product(late_out, late[-1], pairs)
    for copy in copies:
        copy.wait()


def final_sums(flags, lhs, rhs, bases, kinds, divisor, name, late=None):
    hidden_width = lhs[0].shape[0]
    total = len(rhs)
    vmem = pl.BlockSpec(memory_space=pltpu.VMEM)
    outside = pl.BlockSpec(memory_space=pl.ANY)
    operands = [] if late is None else [*late[0], *late[1], late[2]]
    late_total = 0 if late is None else len(late[0])
    operands += lhs
    for parts in rhs:
        operands += parts
    operands += bases
    out_shape = [jax.ShapeDtypeStruct((1, hidden_width, hidden_width), jnp.float32)] * total
    out_specs = [outside] * total
    aliases = {}
    if late is not None:
        out_shape.append(pltpu.VMEM((hidden_width, hidden_width), jnp.float32))
        out_specs.append(vmem)
        aliases = {1 + 2 * late_total: total}
    return pl.pallas_call(
        functools.partial(final_kernel, kinds, len(lhs), late_total, float(divisor)),
        out_shape=out_shape,
        in_specs=[pl.BlockSpec(memory_space=pltpu.SMEM)] + [vmem] * len(operands),
        out_specs=out_specs,
        input_output_aliases=aliases,
        scratch_shapes=[
            pltpu.VMEM((total, hidden_width, hidden_width), jnp.float32),
            pltpu.SemaphoreType.DMA((total, hidden_width // 256)),
        ],
        compiler_params=pltpu.CompilerParams(vmem_limit_bytes=8 << 20),
        cost_estimate=kernel_cost(1 << 20),
        name=name,
    )(flags, *map(in_vmem, operands))


def gathered_shards(
    layer_inputs,
    specialist_picks,
    coefficient_lookup_entry,
    dispatch_coefficients,
    retained_specialist_flags,
    specialist_quotas,
    gating_projection,
    raising_projection,
):
    experts = retained_specialist_flags.shape[0]
    tok_rows, top_count = specialist_picks.shape
    position_ordinal = max(4, 3 * tok_rows * top_count // (4 * experts))
    divisor = experts * position_ordinal

    def onward(x):
        return lax.ppermute(x, "expert", ring_pairs(experts, (1, 1)))

    def backward(x):
        return lax.ppermute(x, "expert", ring_pairs(experts, (-1, -1)))

    def other(x):
        return swapped(x, "expert", 0)

    def stage(arrivals, part, bases, before, after, name, **options):
        blocks, places = [], []
        for block, steps, turn, offset in arrivals:
            blocks.append(block)
            places.append((steps, turn, offset))
            if len(arrivals) > 1:
                blocks.append(other(block))
                places.append((steps, turn ^ 1, offset))
        return run_stage(
            places,
            table,
            retained_specialist_flags,
            blocks,
            gating_projection,
            raising_projection,
            None if part is None else (*part[:3], other(part[3])),
            bases,
            before,
            after,
            name,
            **options,
        )

    tied = lax.optimization_barrier
    left_1, right_1 = onward(layer_inputs), backward(layer_inputs)
    table = route_table(
        specialist_picks, coefficient_lookup_entry, dispatch_coefficients, specialist_quotas
    )
    table = lax.all_to_all(table, "expert", split_axis=0, concat_axis=0, tiled=True)

    table, left_1, right_1 = tied((table, left_1, right_1))
    left_2, right_2 = onward(left_1), backward(right_1)
    first = [(layer_inputs, 0, 0, 0), (left_1, -1, 0, 0), (right_1, 1, 0, 0)]
    first, _ = stage(first, None, None, (), (), "stage_first")

    first, left_2, right_2 = tied((first, left_2, right_2))
    left_3, right_3 = onward(left_2), backward(right_2)
    second = [(left_2, -2, 0, 0), (right_2, 2, 0, 0)]
    second, bases = stage(second, first, None, (0, 1, 2), (0, 1), "stage_second")

    second, bases, left_3, right_3 = tied((second, bases, left_3, right_3))
    far = lax.ppermute(pick_by_core(left_3, right_3), "expert", ring_pairs(experts, (1, -1)))
    third = [(left_3, -3, 0, 0), (right_3, 3, 0, 0)]
    third, bases = stage(third, second, bases, (2,), (0, 1), "stage_third")

    third, bases, far = tied((third, bases, far))
    near_far = other(far)
    mine, _ = stage([(far, 4, 0, 0)], None, None, (), (), "stage_mine", room=2)
    mine, near_far = tied((mine, near_far))
    theirs = [(near_far, 4, 1, 0)]
    last, _ = stage(theirs, None, None, (), (), "stage_theirs", room=2, filled=mine)
    gram, self_cross, merge_base = final_sums(
        retained_specialist_flags,
        [last[0]],
        [[last[1]], [last[2]]],
        bases[:2],
        ("gram", "self"),
        divisor,
        "own_sums",
        ([third[0]], [other(third[3])], bases[2]),
    )
    (merge_cross,) = final_sums(
        retained_specialist_flags,
        [last[0]],
        [[other(last[3])]],
        [merge_base],
        ("merge",),
        divisor,
        "merge_sums",
    )
    return gram, self_cross, merge_cross


def solution(mesh):
    in_specs = (
        P(("parts", "expert", "replica"), None),
        P(("parts", "expert", "replica"), None),
        P(("parts", "expert", "replica"), None),
        P(),
        P(),
        P(),
        P("expert", "replica", None),
        P("expert", "replica", None),
    )
    out_specs = (
        P(("parts", "expert"), "replica", None),
        P(("parts", "expert"), "replica", None),
        P(("parts", "expert"), "replica", None),
    )
    gather_fits = mesh.shape["replica"] == 1 and mesh.shape["expert"] == 16
    body = gathered_shards if gather_fits else shards
    return jax.shard_map(body, mesh=mesh, in_specs=in_specs, out_specs=out_specs, check_vma=False)
```

```python
import functools

import jax
import jax.numpy as jnp
from jax import lax
from jax.experimental import pallas as pl
from jax.experimental.pallas import tpu as pltpu
from jax.sharding import PartitionSpec as P


def swapped(x, axis, stride):
    return lax.ppermute(x, axis, [(i, i ^ 1 << stride) for i in range(lax.axis_size(axis))])


def hidden_rows(slot_rows, w_gate, w_up):
    gate_out = jnp.einsum("nsd,dh->nsh", slot_rows, w_gate, preferred_element_type=jnp.float32)
    upward = jnp.einsum("nsd,dh->nsh", slot_rows, w_up, preferred_element_type=jnp.float32)
    return (jax.nn.silu(gate_out) * upward).astype(jnp.bfloat16)


def weigh_rows(slot_weights, hidden):
    return (slot_weights[..., None].astype(jnp.float32) * hidden.astype(jnp.float32)).astype(
        jnp.bfloat16
    )


def dispatches_at_position(segment_ordinals, specialist_quotas, position_ordinal):
    specialist_sequence = specialist_quotas.shape[0]
    flat_ids = segment_ordinals.reshape(-1)
    route_total = flat_ids.shape[0]
    indicator_vectors = (
        flat_ids[:, None] == jnp.arange(specialist_sequence, dtype=jnp.int32)[None, :]
    ).astype(jnp.int32)
    before = jnp.cumsum(indicator_vectors, axis=0) - indicator_vectors
    route_rank = jnp.sum(before * indicator_vectors, axis=1)
    dispatch_bound = jnp.sum(indicator_vectors * specialist_quotas[None, :], axis=1)
    target = jnp.where(
        route_rank < dispatch_bound,
        flat_ids * position_ordinal + route_rank,
        specialist_sequence * position_ordinal,
    )
    empty_table = jnp.full((specialist_sequence * position_ordinal,), route_total, jnp.int32)
    return empty_table.at[target].set(jnp.arange(route_total, dtype=jnp.int32), mode="drop")


def shards(
    layer_inputs,
    specialist_picks,
    coefficient_lookup_entry,
    dispatch_coefficients,
    retained_specialist_flags,
    specialist_quotas,
    gating_projection,
    raising_projection,
):
    specialist_sequence = retained_specialist_flags.shape[0]
    replica_count = lax.axis_size("replica")
    tok_rows, top_count = specialist_picks.shape
    model_width = layer_inputs.shape[1]
    position_ordinal = max(4, 3 * tok_rows * top_count // (4 * specialist_sequence))
    own_index = lax.axis_index("expert")
    partner_index = jnp.bitwise_xor(own_index, 1)
    expert_lane = jnp.arange(specialist_sequence, dtype=jnp.int32)
    keep_own = jnp.sum(jnp.where(expert_lane == own_index, retained_specialist_flags, 0))
    keep_partner = jnp.sum(jnp.where(expert_lane == partner_index, retained_specialist_flags, 0))
    keep_flag = keep_own.astype(jnp.bfloat16)
    merge_flag = (keep_own * (1 - keep_partner)).astype(jnp.bfloat16)
    gathered_gate, gathered_up = (
        lax.all_gather(gating_projection, "replica", axis=1, tiled=True),
        lax.all_gather(raising_projection, "replica", axis=1, tiled=True),
    )
    w_gate = gathered_gate[0]
    w_up = gathered_up[0]
    dispatch_sequence = dispatches_at_position(
        specialist_picks, specialist_quotas, position_ordinal
    )
    route_total = tok_rows * top_count
    token_slot = jnp.where(
        dispatch_sequence < route_total, dispatch_sequence // top_count, tok_rows
    )
    padded_tokens = jnp.concatenate(
        [layer_inputs, jnp.zeros((1, model_width), layer_inputs.dtype)], axis=0
    )
    send_rows = padded_tokens[token_slot].reshape(
        specialist_sequence, position_ordinal, model_width
    )
    levels = dispatch_coefficients.shape[0]
    onehot_levels = (
        coefficient_lookup_entry.reshape(-1)[:, None]
        == jnp.arange(levels, dtype=jnp.int32)[None, :]
    ).astype(jnp.bfloat16)
    route_weights = jnp.dot(
        onehot_levels, dispatch_coefficients, preferred_element_type=jnp.float32
    )
    padded_weights = jnp.concatenate([route_weights, jnp.zeros((1,), jnp.float32)], axis=0)
    send_weights = (
        padded_weights[dispatch_sequence]
        .astype(jnp.bfloat16)
        .reshape(specialist_sequence, position_ordinal)
    )
    slot_rows = lax.all_to_all(send_rows, "expert", split_axis=0, concat_axis=0, tiled=True)
    slot_weights = lax.all_to_all(send_weights, "expert", split_axis=0, concat_axis=0, tiled=True)
    own_hidden = hidden_rows(slot_rows, w_gate, w_up)
    arrived, own_hidden, own_weighted = (
        slot_rows,
        own_hidden,
        weigh_rows(slot_weights, own_hidden),
    )
    partner_rows, incoming = swapped((arrived, own_weighted), "expert", 0)
    crossed = hidden_rows(partner_rows, w_gate, w_up)
    hidden_width = own_hidden.shape[-1]
    own_flat = (own_hidden * keep_flag).reshape(-1, hidden_width)
    weighted_flat = own_weighted.reshape(-1, hidden_width)
    crossed_flat = (crossed * merge_flag).reshape(-1, hidden_width)
    incoming_flat = incoming.reshape(-1, hidden_width)
    both_rows = jnp.concatenate([own_flat, crossed_flat], axis=0)
    gram_part = jnp.einsum("mi,mj->ij", both_rows, both_rows, preferred_element_type=jnp.float32)
    self_part = jnp.einsum("mi,mj->ij", own_flat, weighted_flat, preferred_element_type=jnp.float32)
    merge_part = jnp.einsum(
        "mi,mj->ij", crossed_flat, incoming_flat, preferred_element_type=jnp.float32
    )
    shared_rows = lax.psum_scatter(
        jnp.concatenate([gram_part, self_part, merge_part], axis=1),
        "replica",
        scatter_dimension=0,
        tiled=True,
    )
    slot_total = jnp.float32(replica_count * specialist_sequence * position_ordinal)
    shared_rows = shared_rows / slot_total
    gram = shared_rows[:, :hidden_width]
    self_cross = shared_rows[:, hidden_width : 2 * hidden_width]
    merge_cross = shared_rows[:, 2 * hidden_width :]
    return (gram[None], self_cross[None], merge_cross[None])


def kernel_cost(flops):
    return pl.CostEstimate(flops=flops, bytes_accessed=1 << 16, transcendentals=0)


def in_hbm(x):
    return pltpu.with_memory_space_constraint(x, pltpu.HBM)


def route_table_kernel(
    quota_in, flag_in, pick_in, entry_in, coef_in, out_ref, mark_ref, *scratch
):
    quota_ref, flag_ref, pick_ref, entry_ref, coef_ref, arrive = scratch
    copies = [
        pltpu.make_async_copy(pick_in, pick_ref, arrive.at[0]),
        pltpu.make_async_copy(entry_in, entry_ref, arrive.at[1]),
        pltpu.make_async_copy(coef_in, coef_ref, arrive.at[2]),
        pltpu.make_async_copy(quota_in, quota_ref, arrive.at[3]),
        pltpu.make_async_copy(flag_in, flag_ref, arrive.at[4]),
    ]
    for copy in copies:
        copy.start()
    for copy in copies:
        copy.wait()
    top_count, tokens = pick_ref.shape
    experts = out_ref.shape[0]
    levels = coef_ref.shape[0]
    picks = pick_ref[...]
    entries = entry_ref[...]
    coef = coef_ref[...].reshape(1, levels)
    expert_row = lax.broadcasted_iota(jnp.int32, (experts, tokens), 0)
    level_row = lax.broadcasted_iota(jnp.int32, (levels, tokens), 0)
    chosen = jnp.zeros((experts, tokens), jnp.float32)
    weight = jnp.zeros((experts, tokens), jnp.float32)
    for choice in range(top_count):
        level = jnp.where(entries[choice : choice + 1, :] == level_row, 1.0, 0.0)
        value = jnp.dot(coef, level.astype(jnp.bfloat16), preferred_element_type=jnp.float32)
        hit = picks[choice : choice + 1, :] == expert_row
        chosen = jnp.where(hit, 1.0, chosen)
        weight = jnp.where(hit, value, weight)
    row = lax.broadcasted_iota(jnp.int32, (tokens, tokens), 0)
    col = lax.broadcasted_iota(jnp.int32, (tokens, tokens), 1)
    earlier = jnp.where(row < col, 1.0, 0.0).astype(jnp.bfloat16)
    rank = jnp.dot(chosen.astype(jnp.bfloat16), earlier, preferred_element_type=jnp.float32)
    bound = jnp.zeros((experts, tokens), jnp.float32)
    for expert in range(experts):
        bound = jnp.where(expert_row == expert, quota_ref[expert].astype(jnp.float32), bound)
    used = jnp.where(rank < bound, weight, 0.0).astype(jnp.bfloat16)
    me = lax.axis_index("expert")
    keep = flag_ref[me].astype(jnp.float32)
    merge = keep * (1.0 - flag_ref[jnp.bitwise_xor(me, 1)].astype(jnp.float32))
    mark_row = lax.broadcasted_iota(jnp.int32, mark_ref.shape, 0)
    mark_ref[...] = jnp.where(mark_row == 0, keep, merge)
    for receiver in range(experts):
        out_ref[receiver, 0:1, :] = used[receiver : receiver + 1]
        out_ref[receiver, 1:2, :] = used[receiver ^ 1 : (receiver ^ 1) + 1]


def route_table(picks, entries, coefficients, quotas, flags):
    experts = quotas.shape[0]
    tokens = picks.shape[0]
    vmem = pl.BlockSpec(memory_space=pltpu.VMEM)
    outside = pl.BlockSpec(memory_space=pl.ANY)
    return pl.pallas_call(
        route_table_kernel,
        out_shape=(
            jax.ShapeDtypeStruct((experts, 2, tokens), jnp.bfloat16),
            pltpu.VMEM((8, 128), jnp.float32),
        ),
        in_specs=[outside] * 5,
        out_specs=(vmem, vmem),
        scratch_shapes=[
            pltpu.SMEM(quotas.shape, quotas.dtype),
            pltpu.SMEM(flags.shape, flags.dtype),
            pltpu.VMEM(picks.shape[::-1], jnp.int32),
            pltpu.VMEM(entries.shape[::-1], jnp.int32),
            pltpu.VMEM(coefficients.shape, coefficients.dtype),
            pltpu.SemaphoreType.DMA((5,)),
        ],
        compiler_params=pltpu.CompilerParams(vmem_limit_bytes=4 << 20),
        cost_estimate=kernel_cost(1 << 34),
        name="route_table",
    )(*map(in_hbm, (quotas, flags, picks.T, entries.T, coefficients)))


def ring_neighbour(me, experts, steps, turn):
    rows = experts // 4
    row, side, core = me // 4, jnp.bitwise_and(me // 2, 1), jnp.bitwise_and(me, 1)
    position = jnp.where(side == 0, row, 2 * rows - 1 - row)
    position = lax.rem(position + steps + 2 * rows, 2 * rows)
    far = position >= rows
    row = jnp.where(far, 2 * rows - 1 - position, position)
    return 4 * row + jnp.where(far, 2, 0) + jnp.bitwise_xor(core, turn)


def ring_pairs(experts, directions):
    rows = experts // 4
    chips = [2 * row for row in range(rows)] + [2 * row + 1 for row in reversed(range(rows))]
    return [
        (2 * chip + core, 2 * chips[(position + directions[core]) % len(chips)] + core)
        for position, chip in enumerate(chips)
        for core in range(2)
    ]


def stage_kernel(places, before, after, with_base, rows_at, *refs):
    taken = iter(refs)

    def take(count):
        return [next(taken) for _ in range(count)]

    table_ref, mark_ref = take(2)
    blocks = take(len(places))
    weights = take(2)
    part = take(4) if before else None
    sum_total = max((*before, *after), default=-1) + 1
    bases = take(sum_total) if with_base else [None] * 3
    take(4 if rows_at else 0)
    hidden_outs = take(4)
    sums = take(sum_total)
    scratch = take(2)
    for which in before:
        add_product(sums[which], bases[which], [(part[0], part[1 + which])])
    hidden_body(places, rows_at, table_ref, mark_ref, blocks, *weights, *hidden_outs, *scratch)
    for which in after:
        base = sums[which] if which in before else bases[which]
        add_product(sums[which], base, [(hidden_outs[0], hidden_outs[1 + which])])


def add_product(out_ref, base_ref, pairs):
    hidden_width = out_ref.shape[1]
    tile = 256
    for start in range(0, hidden_width, tile):
        lanes = slice(start, start + tile)
        total = None if base_ref is None else base_ref[:, lanes]
        for lhs_ref, rhs_ref in pairs:
            term = jnp.dot(lhs_ref[...], rhs_ref[:, lanes], preferred_element_type=jnp.float32)
            total = term if total is None else total + term
        out_ref[:, lanes] = total


def hidden_body(
    places,
    rows_at,
    table_ref,
    mark_ref,
    block_refs,
    gate_ref,
    up_ref,
    lhs_ref,
    count_ref,
    weigh_ref,
    send_ref,
    rows_ref,
    coef_ref,
):
    block_total = len(places)
    experts, _, tokens = table_ref.shape
    hidden_width = gate_ref.shape[2]
    spans = []
    for block in range(block_total):
        first = spans[-1].stop if spans else 0
        spans.append(slice(first, first + block_refs[block].shape[0]))
        rows_ref[spans[block], :] = block_refs[block][...]
    me = lax.axis_index("expert")
    keep, merge = mark_ref[0:1, 0:1], mark_ref[1:2, 0:1]
    row = lax.broadcasted_iota(jnp.int32, (tokens, tokens), 0)
    col = lax.broadcasted_iota(jnp.int32, (tokens, tokens), 1)
    for block, (steps, turn, offset) in enumerate(places):
        source = ring_neighbour(me, experts, steps, turn)
        table = table_ref[source].astype(jnp.float32)
        own = jnp.sum(jnp.where(row == col, table[0:1], 0.0), axis=1, keepdims=True)
        partner = jnp.sum(jnp.where(row == col, table[1:2], 0.0), axis=1, keepdims=True)
        count = jnp.where(own > 0.0, keep, 0.0) + jnp.where(partner > 0.0, merge, 0.0)
        size = spans[block].stop - spans[block].start
        part = slice(offset, offset + size)
        coef_ref[0, spans[block], :] = jnp.broadcast_to(count[part], (size, 128))
        coef_ref[1, spans[block], :] = jnp.broadcast_to(own[part], (size, 128))
    tile = 256
    units = [(0,)] if block_total == 1 else [(i, i + 1) for i in range(0, block_total, 2)]
    groups, group = [], []
    for unit in units:
        group.append(unit)
        if spans[unit[-1]].stop - spans[group[0][0]].start >= 256 or unit == units[-1]:
            groups.append(group)
            group = []
    for group in groups:
        span = slice(spans[group[0][0]].start, spans[group[-1][-1]].stop)
        rows = rows_ref[span, :]
        for start in range(0, hidden_width, tile):
            lanes = slice(start, start + tile)
            gate = jnp.dot(rows, gate_ref[0, :, lanes], preferred_element_type=jnp.float32)
            upward = jnp.dot(rows, up_ref[0, :, lanes], preferred_element_type=jnp.float32)
            hidden = (gate / (1.0 + jnp.exp(-gate)) * upward).astype(jnp.bfloat16)
            out_span = slice(span.start + rows_at, span.stop + rows_at)
            lhs_ref[lanes, out_span] = hidden.T
            hidden = hidden.astype(jnp.float32)
            for lane in range(0, tile, 128):
                part = hidden[:, lane : lane + 128]
                to = slice(start + lane, start + lane + 128)
                count_ref[out_span, to] = (part * coef_ref[0, span, :]).astype(jnp.bfloat16)
                weighed = (part * coef_ref[1, span, :]).astype(jnp.bfloat16)
                weigh_ref[out_span, to] = weighed
                if block_total == 1:
                    send_at = send_ref.shape[0] - span.stop - rows_at
                    send_ref[send_at : send_at + span.stop, to] = weighed
                    continue
                for unit in group:
                    for block, source in zip(unit, unit[::-1]):
                        base = span.start
                        piece = slice(spans[source].start - base, spans[source].stop - base)
                        send_ref[spans[block], to] = weighed[piece]


def in_vmem(x):
    return pltpu.with_memory_space_constraint(x, pltpu.VMEM)


def run_stage(
    places, table, marks, blocks, w_gate, w_up, part, bases, before, after, name, room=1, filled=None
):
    width = blocks[0].shape[1]
    rows = sum(block.shape[0] for block in blocks)
    hidden_width = w_gate.shape[2]
    vmem = pl.BlockSpec(memory_space=pltpu.VMEM)
    operands = [in_vmem(table), in_vmem(marks), *map(in_vmem, blocks), in_vmem(w_gate), in_vmem(w_up)]
    out_shape = [
        pltpu.VMEM((hidden_width, room * rows), jnp.bfloat16),
        pltpu.VMEM((room * rows, hidden_width), jnp.bfloat16),
        pltpu.VMEM((room * rows, hidden_width), jnp.bfloat16),
        pltpu.VMEM((room * rows, hidden_width), jnp.bfloat16),
    ]
    aliases = {}
    if before:
        operands += map(in_vmem, part)
    sum_total = max((*before, *after), default=-1) + 1
    out_shape += [pltpu.VMEM((hidden_width, hidden_width), jnp.float32)] * sum_total
    if bases is not None:
        aliases = {len(operands) + index: 4 + index for index in range(sum_total)}
        operands += map(in_vmem, bases)
    if filled is not None:
        aliases |= {len(operands) + index: index for index in range(4)}
        operands += map(in_vmem, filled)
    in_specs = [vmem] * len(operands)
    outs = pl.pallas_call(
        functools.partial(
            stage_kernel, places, before, after, bases is not None, 0 if filled is None else rows
        ),
        out_shape=out_shape,
        in_specs=in_specs,
        out_specs=[vmem] * len(out_shape),
        input_output_aliases=aliases,
        scratch_shapes=[
            pltpu.VMEM((rows, width), jnp.bfloat16),
            pltpu.VMEM((2, rows, 128), jnp.float32),
        ],
        compiler_params=pltpu.CompilerParams(vmem_limit_bytes=10 << 20),
        cost_estimate=kernel_cost(4 * rows * width * hidden_width),
        name=name,
    )(*operands)
    return tuple(outs[:4]), tuple(outs[4:])


def pick_kernel(even_ref, odd_ref, out_ref):
    core = jnp.bitwise_and(lax.axis_index("expert"), 1)

    @pl.when(core == 0)
    def _():
        out_ref[...] = even_ref[...]

    @pl.when(core == 1)
    def _():
        out_ref[...] = odd_ref[...]


def pick_by_core(even, odd):
    vmem = pl.BlockSpec(memory_space=pltpu.VMEM)
    return pl.pallas_call(
        pick_kernel,
        out_shape=pltpu.VMEM(even.shape, even.dtype),
        in_specs=[vmem, vmem],
        out_specs=vmem,
        compiler_params=pltpu.CompilerParams(vmem_limit_bytes=4 << 20),
        name="pick_by_core",
    )(in_vmem(even), in_vmem(odd))


def final_kernel(kinds, part_total, late_total, divisor, mark_ref, *refs):
    set_total = len(kinds)
    if late_total:
        late, refs = refs[: 2 * late_total + 1], refs[2 * late_total + 1 :]
        late_out = refs[-3]
        refs = refs[:-3] + refs[-2:]
    lhs, rest = refs[:part_total], refs[part_total:]
    rhs = [rest[part_total * index : part_total * (index + 1)] for index in range(set_total)]
    rest = rest[part_total * set_total :]
    bases, outs = rest[:set_total], rest[set_total : 2 * set_total]
    done_ref, leave = rest[2 * set_total :]
    hidden_width = lhs[0].shape[0]
    tile = 256
    copies = []
    for index in range(set_total):
        factor = 1.0 / divisor
        if kinds[index] != "gram":
            mark = 0 if kinds[index] == "self" else 1
            factor = factor * mark_ref[mark : mark + 1, 0:1]
        for start in range(0, hidden_width, tile):
            span = slice(start, start + tile)
            total = bases[index][span, :]
            for left, right in zip(lhs, rhs[index]):
                total = total + jnp.dot(
                    left[span, :], right[...], preferred_element_type=jnp.float32
                )
            done_ref[index, span, :] = total * factor
            copies.append(
                pltpu.make_async_copy(
                    done_ref.at[index, span],
                    outs[index].at[0, span],
                    leave.at[index, start // tile],
                )
            )
            copies[-1].start()
    if late_total:
        pairs = [(late[index], late[late_total + index]) for index in range(late_total)]
        add_product(late_out, late[-1], pairs)
    for copy in copies:
        copy.wait()


def final_sums(marks, lhs, rhs, bases, kinds, divisor, name, late=None):
    hidden_width = lhs[0].shape[0]
    total = len(rhs)
    vmem = pl.BlockSpec(memory_space=pltpu.VMEM)
    outside = pl.BlockSpec(memory_space=pl.ANY)
    operands = [] if late is None else [*late[0], *late[1], late[2]]
    late_total = 0 if late is None else len(late[0])
    operands += lhs
    for parts in rhs:
        operands += parts
    operands += bases
    out_shape = [jax.ShapeDtypeStruct((1, hidden_width, hidden_width), jnp.float32)] * total
    out_specs = [outside] * total
    aliases = {}
    if late is not None:
        out_shape.append(pltpu.VMEM((hidden_width, hidden_width), jnp.float32))
        out_specs.append(vmem)
        aliases = {1 + 2 * late_total: total}
    return pl.pallas_call(
        functools.partial(final_kernel, kinds, len(lhs), late_total, float(divisor)),
        out_shape=out_shape,
        in_specs=[vmem] * (1 + len(operands)),
        out_specs=out_specs,
        input_output_aliases=aliases,
        scratch_shapes=[
            pltpu.VMEM((total, hidden_width, hidden_width), jnp.float32),
            pltpu.SemaphoreType.DMA((total, hidden_width // 256)),
        ],
        compiler_params=pltpu.CompilerParams(vmem_limit_bytes=8 << 20),
        cost_estimate=kernel_cost(1 << 20),
        name=name,
    )(in_vmem(marks), *map(in_vmem, operands))


def gathered_shards(
    layer_inputs,
    specialist_picks,
    coefficient_lookup_entry,
    dispatch_coefficients,
    retained_specialist_flags,
    specialist_quotas,
    gating_projection,
    raising_projection,
):
    experts = retained_specialist_flags.shape[0]
    tok_rows, top_count = specialist_picks.shape
    position_ordinal = max(4, 3 * tok_rows * top_count // (4 * experts))
    divisor = experts * position_ordinal

    def onward(x):
        return lax.ppermute(x, "expert", ring_pairs(experts, (1, 1)))

    def backward(x):
        return lax.ppermute(x, "expert", ring_pairs(experts, (-1, -1)))

    def other(x):
        return swapped(x, "expert", 0)

    def stage(arrivals, part, bases, before, after, name, **options):
        blocks, places = [], []
        for block, steps, turn, offset in arrivals:
            blocks.append(block)
            places.append((steps, turn, offset))
            if len(arrivals) > 1:
                blocks.append(other(block))
                places.append((steps, turn ^ 1, offset))
        return run_stage(
            places,
            table,
            marks,
            blocks,
            gating_projection,
            raising_projection,
            None if part is None else (*part[:3], other(part[3])),
            bases,
            before,
            after,
            name,
            **options,
        )

    tied = lax.optimization_barrier
    left_1, right_1 = onward(layer_inputs), backward(layer_inputs)
    table, marks = route_table(
        specialist_picks,
        coefficient_lookup_entry,
        dispatch_coefficients,
        specialist_quotas,
        retained_specialist_flags,
    )
    table = lax.all_to_all(table, "expert", split_axis=0, concat_axis=0, tiled=True)

    table, left_1, right_1 = tied((table, left_1, right_1))
    left_2, right_2 = onward(left_1), backward(right_1)
    first = [(layer_inputs, 0, 0, 0), (left_1, -1, 0, 0), (right_1, 1, 0, 0)]
    first, _ = stage(first, None, None, (), (), "stage_first")

    first, left_2, right_2 = tied((first, left_2, right_2))
    left_3, right_3 = onward(left_2), backward(right_2)
    second = [(left_2, -2, 0, 0), (right_2, 2, 0, 0)]
    second, bases = stage(second, first, None, (0, 1, 2), (0, 1), "stage_second")

    second, bases, left_3, right_3 = tied((second, bases, left_3, right_3))
    far = lax.ppermute(pick_by_core(left_3, right_3), "expert", ring_pairs(experts, (1, -1)))
    third = [(left_3, -3, 0, 0), (right_3, 3, 0, 0)]
    third, bases = stage(third, second, bases, (2,), (0, 1), "stage_third")

    third, bases, far = tied((third, bases, far))
    near_far = other(far)
    mine, _ = stage([(far, 4, 0, 0)], None, None, (), (), "stage_mine", room=2)
    mine, near_far = tied((mine, near_far))
    theirs = [(near_far, 4, 1, 0)]
    last, _ = stage(theirs, None, None, (), (), "stage_theirs", room=2, filled=mine)
    gram, self_cross, merge_base = final_sums(
        marks,
        [last[0]],
        [[last[1]], [last[2]]],
        bases[:2],
        ("gram", "self"),
        divisor,
        "own_sums",
        ([third[0]], [other(third[3])], bases[2]),
    )
    (merge_cross,) = final_sums(
        marks,
        [last[0]],
        [[other(last[3])]],
        [merge_base],
        ("merge",),
        divisor,
        "merge_sums",
    )
    return gram, self_cross, merge_cross


def solution(mesh):
    in_specs = (
        P(("parts", "expert", "replica"), None),
        P(("parts", "expert", "replica"), None),
        P(("parts", "expert", "replica"), None),
        P(),
        P(),
        P(),
        P("expert", "replica", None),
        P("expert", "replica", None),
    )
    out_specs = (
        P(("parts", "expert"), "replica", None),
        P(("parts", "expert"), "replica", None),
        P(("parts", "expert"), "replica", None),
    )
    gather_fits = mesh.shape["replica"] == 1 and mesh.shape["expert"] == 16
    body = gathered_shards if gather_fits else shards
    return jax.shard_map(body, mesh=mesh, in_specs=in_specs, out_specs=out_specs, check_vma=False)
```
